256 devices in a mesh: band: 16 (over x_lo, y, core), chan: 16 (over z, x_hi).
Axes of the slice: x: 4 (x_hi: 2, x_lo: 2; x = x_hi * 2 + x_lo), y: 4, z: 8, core: 2. Of those that a mesh axis runs over, the one named last changes fastest.
Arguments:
- inputs: bfloat16 [256, 256, 384], P('chan', 'band'), may hold values from -6 to 6
- cotangent: bfloat16 [256, 256, 384], P('chan', 'band'), may hold values from -6 to 6
- kernel: bfloat16 [256, 3, 3, 256], P('chan'), may hold values from -0.125 to 0.125
- channel_bias: float32 [256], P('chan'), may hold values from -4 to 4
Outputs:
- input_grad: bfloat16 [256, 256, 384], P('chan', 'band')
- kernel_grad: float32 [256, 3, 3, 256], P('chan')
The draws below stay inside these ranges and needn't reach their ends.
All inputs are finite; a program needn't handle non-finite values.
Results may differ from the reference program's by a relative error of at most 0.0095.
Values may be sent and summed in bfloat16 or wider, within the bound.
No kernel may reach another device: no remote copies, remote signals or barrier semaphores. Data moves between devices by JAX's collectives and lax.ppermute only.
A program may use at most 128 MiB of HBM per device.

```python
import math
import jax
import jax.numpy as jnp

C = 256
COLS = 384
LAT = 256


def shard_levels(rng, dims, split, low, largest):
    loudness, own = 1.0, jax.random.fold_in(rng, 6)
    for axis_at, shards_of in split:
        heights = jnp.exp(jax.random.uniform(jax.random.fold_in(own, axis_at), (shards_of,), jnp.float32, low / len(split), largest / len(split)))
        loudness = loudness * jnp.repeat(heights, dims[axis_at] // shards_of).reshape([-1 if axis == axis_at else 1 for axis in range(len(dims))])
    return loudness


def centred(own_key, extent, deviation, reach, split=(), kind=jnp.bfloat16):
    factor_of = shard_levels(own_key, extent, split, -0.22, 0.18) if split else 1.0
    result = jax.random.normal(own_key, extent, jnp.float32) * deviation * factor_of
    return jnp.minimum(jnp.maximum(result, -reach), reach).astype(kind)


def setup_inputs(seed: int = 0) -> dict:
    key_of = jax.random.split(jax.random.key(seed), 5)
    return {
        "inputs": centred(key_of[0], (C, LAT, COLS), 1.0, 6.0, ((0, 16), (1, 16))),
        "cotangent": centred(key_of[1], (C, LAT, COLS), 1.0, 6.0, ((0, 16), (1, 16))),
        "kernel": centred(key_of[2], (C, 3, 3, C), (9 * C) ** -0.5, 0.125, ((0, 16),)),
        "channel_bias": centred(key_of[3], (C,), 1.0, 4.0, ((0, 16),), jnp.float32),
    }


def reference(inputs, cotangent, kernel, channel_bias):
    height = inputs.shape[1]
    width = inputs.shape[2]
    kernel_f = kernel.astype(jnp.float32)
    padded_in = jnp.pad(inputs.astype(jnp.float32), ((0, 0), (1, 1), (1, 1)))
    pre = jnp.zeros((kernel.shape[0], height, width), jnp.float32) + channel_bias[:, None, None]
    for row_tap in range(3):
        for col_tap in range(3):
            pre = pre + jnp.einsum('oi,ihw->ohw', kernel_f[:, row_tap, col_tap, :], padded_in[:, row_tap:row_tap + height, col_tap:col_tap + width])
    sigmo = jax.nn.sigmoid(pre)
    grad_pre = (cotangent.astype(jnp.float32) * sigmo * (1.0 + pre * (1.0 - sigmo))).astype(jnp.bfloat16)
    grad_f = grad_pre.astype(jnp.float32)
    padded_grad = jnp.pad(grad_f, ((0, 0), (1, 1), (1, 1)))
    input_grad = jnp.zeros(inputs.shape, jnp.float32)
    taps = []
    for row_tap in range(3):
        for col_tap in range(3):
            input_grad = input_grad + jnp.einsum('oi,ohw->ihw', kernel_f[:, row_tap, col_tap, :], padded_grad[:, 2 - row_tap:2 - row_tap + height, 2 - col_tap:2 - col_tap + width])
            taps.append(jnp.einsum('ohw,ihw->oi', grad_f, padded_in[:, row_tap:row_tap + height, col_tap:col_tap + width]))
    factor = 1.0 / math.sqrt(height * width)
    kernel_grad = jnp.stack(taps, axis=1).reshape(kernel.shape) * factor
    return (input_grad.astype(jnp.bfloat16), kernel_grad)
```

```python
import math

import jax
import jax.numpy as jnp
from jax import lax
from jax.experimental import pallas as pl
from jax.experimental.pallas import tpu as pltpu
from jax.sharding import Mesh
from jax.sharding import PartitionSpec as P

BF = jnp.bfloat16
F32 = jnp.float32
CHAN = ("z", "xh")
BAND = ("xl", "y", "core")
PITCH = 32
NCOL = 24
PX = 1152
NT = (((1,), (1,)), ((), ()))
TN = (((0,), (0,)), ((), ()))


def dot(a, b, dims=(((1,), (0,)), ((), ()))):
    return lax.dot_general(a, b, dims, preferred_element_type=F32)


def iota(shape, dim):
    return lax.broadcasted_iota(jnp.int32, shape, dim)


def call(body, outs, *args, smem=True, scratch=()):
    specs = [pl.BlockSpec(memory_space=pltpu.VMEM)] * len(args)
    if smem:
        specs[0] = pl.BlockSpec(memory_space=pltpu.SMEM)
    return pl.pallas_call(
        body,
        out_shape=[jax.ShapeDtypeStruct(s, d) for s, d in outs],
        in_specs=specs,
        out_specs=[pl.BlockSpec(memory_space=pltpu.VMEM)] * len(outs),
        scratch_shapes=list(scratch),
        compiler_params=pltpu.CompilerParams(vmem_limit_bytes=48 * 1024 * 1024),
    )(*args)


def swap_blocks(arrays, block):
    lanes = arrays[0].shape[1]
    place = iota(arrays[0].shape, 1) // block
    bit = 1
    while bit < len(arrays):
        upper = (place & bit) != 0
        out = list(arrays)
        for s in range(len(arrays)):
            if s & bit:
                continue
            a, b = arrays[s], arrays[s | bit]
            out[s] = jnp.where(upper, pltpu.roll(b, bit * block, 1), a)
            out[s | bit] = jnp.where(upper, b, pltpu.roll(a, lanes - bit * block, 1))
        arrays = out
        bit *= 2
    return arrays


def window(first, count):
    row = iota((512, 384), 0)
    c = row & 31
    hit = (iota((512, 384), 1) == (row >> 5) * NCOL + c + first) & (c < count)
    return jnp.where(hit, 1.0, 0.0).astype(BF)


def pack_kernel(core_ref, x_ref, cot_ref, ker_ref, bias_ref, out_ref):
    core = core_ref[0]
    src = iota((256, 256), 0)
    dst = iota((256, 256), 1)
    ch, h = src >> 4, src & 15
    to_h_ch = jnp.where(dst == h * 16 + ch, 1.0, 0.0).astype(BF)
    other = (ch >> 3) ^ core
    to_half = jnp.where(dst == other * 128 + h * 8 + (ch & 7), 1.0, 0.0).astype(BF)

    x = dot(window(-2, 28), x_ref[...].reshape(256, 384), NT).astype(BF)
    x = dot(x, to_h_ch).astype(BF).reshape(16, 32, 256)
    out_ref[:, 0:32, :] = x[:, :, 0:128]
    out_ref[:, 32:64, :] = x[:, :, 128:256]

    bias = jnp.broadcast_to(bias_ref[...], (8, 16))
    hi = bias.astype(BF).astype(F32)
    mid = (bias - hi).astype(BF).astype(F32)
    low = bias - hi - mid
    k = iota((8, 16), 0)
    pieces = jnp.where(k == 4, hi, jnp.where(k == 5, mid, jnp.where(k == 6, low, 0.0)))
    spread = iota((16, 128), 0) == (core * 8 + (iota((16, 128), 1) & 7))
    pieces = dot(pieces.astype(BF), jnp.where(spread, 1.0, 0.0).astype(BF))
    rows = jnp.concatenate([jnp.zeros((24, 128), F32), pieces], axis=0)

    c = dot(window(-1, 26), cot_ref[...].reshape(256, 384), NT).astype(BF)
    c = dot(c, to_half).reshape(16, 32, 256)
    out_ref[:, 64:96, :] = (c[:, :, 0:128] + rows[None]).astype(BF)
    out_ref[:, 96:128, :] = c[:, :, 128:256].astype(BF)

    parts = []
    for t in range(9):
        both = ker_ref[t].astype(F32)
        mine = jnp.where(core == 0, both[0:8], both[8:16])
        parts += [mine[:, 0:128], mine[:, 128:256]]
    weights = jnp.concatenate(parts, axis=0).astype(BF)
    for j in range(16):
        out_ref[j, 128:272, :] = weights


def unpack_kernel(core_ref, r_ref, xo_ref, co_ref, ha_ref, hb_ref, w_ref):
    core = core_ref[0]
    edge = []
    for hh in range(2):
        halves = []
        for sh in range(2):
            got = [r_ref[sh * 8 + s, hh * 32 : hh * 32 + 32, :] for s in range(8)]
            halves.append(swap_blocks(got, 16))
        for hl in range(8):
            at = (hh * 8 + hl) * 32
            row = jnp.concatenate([halves[0][hl], halves[1][hl]], axis=1)
            xo_ref[at : at + 32, :] = row
            if (hh * 8 + hl) in (0, 1, 14, 15):
                edge.append(row)
    own = swap_blocks([r_ref[s, 64:96, :] for s in range(16)], 8)
    oth = swap_blocks([r_ref[s, 96:128, :] for s in range(16)], 8)
    for h in range(16):
        co_ref[h * 32 : h * 32 + 32, :] = own[h]
        at = 512 + (h % 8) * 32
        xo_ref[at : at + 32, (h // 8) * 128 : (h // 8) * 128 + 128] = oth[h]
    first = core == 0
    blank = jnp.zeros((32, 128), BF)
    for ref, cot in ((ha_ref, oth), (hb_ref, own)):
        ref[0:32, :] = jnp.where(first, edge[0], edge[2])
        ref[32:64, :] = jnp.where(first, edge[1], edge[3])
        ref[64:96, 0:128] = jnp.where(first, cot[0], cot[15])
        ref[64:96, 128:256] = blank
    chunks = [r_ref[s, 128:272, :].astype(F32) for s in range(16)]
    for t in range(9):
        for ih in range(2):
            at = (t * 2 + ih) * 8
            tap = jnp.concatenate([c[at : at + 8] for c in chunks], axis=0)
            w_ref[t * 128 : t * 128 + 128, ih * 128 : ih * 128 + 128] = tap.astype(BF)


def grad_kernel(
    scale, core_ref, xo_ref, xr_ref, co_ref, ha_ref, hb_ref, w_ref, kg_ref, g_ref, x, cot, y, gs
):
    core = core_ref[0]
    first = core == 0
    mine = pl.multiple_of(core * 512, 512)
    theirs = pl.multiple_of((1 - core) * 512, 512)
    x[0:64, :] = jnp.where(first, ha_ref[0:64, :], hb_ref[0:64, :])
    x[pl.ds(64 + mine, 512), :] = xo_ref[0:512, :]
    x[pl.ds(64 + theirs, 512), :] = xr_ref[0:512, :]
    x[1088:1152, :] = jnp.where(first, hb_ref[0:64, :], ha_ref[0:64, :])
    x[1152:1216, :] = jnp.zeros((64, 256), BF)
    cot[0:32, :] = jnp.where(first, ha_ref[64:96, 0:128], hb_ref[64:96, 0:128])
    cot[pl.ds(32 + mine, 512), :] = co_ref[...]
    cot[pl.ds(32 + theirs, 256), :] = xr_ref[512:768, 0:128]
    cot[pl.ds(32 + theirs + 256, 256), :] = xr_ref[512:768, 128:256]
    cot[1056:1088, :] = jnp.where(first, hb_ref[64:96, 0:128], ha_ref[64:96, 0:128])

    bias = co_ref[16:32, :].astype(F32)
    bias = bias[12:13] + bias[13:14] + bias[14:15]

    for m in range(0, PX, 384):
        y[m : m + 384, :] = (
            dot(x[m : m + 384, :], w_ref[0:384, :], NT)
            + dot(x[m + 32 : m + 416, :], w_ref[384:768, :], NT)
            + dot(x[m + 64 : m + 448, :], w_ref[768:1152, :], NT)
        )

    gs[0:16, :] = jnp.zeros((16, 128), F32)
    for m in range(0, 1088, 64):
        pre = (
            y[m : m + 64, 0:128]
            + y[m + 1 : m + 65, 128:256]
            + y[m + 2 : m + 66, 256:384]
            + bias
        )
        s = 1.0 / (1.0 + jnp.exp(-pre))
        c = iota((64, 128), 0) & 31
        grad = cot[m : m + 64, :].astype(F32) * s * (1.0 + pre * (1.0 - s))
        grad = jnp.where(c < 26, grad, 0.0).astype(BF)
        g_ref[m : m + 64, :] = grad
        p = iota((64, 128), 0) + m
        inner = (c >= 1) & (c <= NCOL) & (p >= 32) & (p < 1056)
        gs[16 + m : 16 + m + 64, :] = jnp.where(inner, grad.astype(F32), 0.0)
    g_ref[1088:PX, :] = jnp.zeros((PX - 1088, 128), BF)
    gs[16 + 1088 : 16 + PX, :] = jnp.zeros((PX - 1088, 128), F32)

    taps = []
    shifted = jnp.concatenate(
        [gs[16 - b : 16 - b + PX, :].astype(BF) for b in range(3)], axis=1
    )
    for a in range(3):
        block = dot(shifted, x[32 * a : 32 * a + PX, :], TN) * scale
        taps += [block[0:128], block[128:256], block[256:384]]
    for m in range(8):
        lane = (m // 4) * 128
        for j in range(16):
            o = slice(8 * j, 8 * j + 8)
            kg_ref[m * 16 + j] = jnp.concatenate(
                [taps[m][o, 0:128], taps[m][o, 128:256], taps[8][o, lane : lane + 128]], axis=0
            ).astype(BF)


def input_kernel(core_ref, g_ref, w_ref, own_ref, send_ref, z, total):
    core = core_ref[0]
    for m in (0, 352, 704):
        for b in range(3):
            z[b, m : m + 352, :] = (
                dot(g_ref[m + 64 : m + 416, :], w_ref[b * 128 : b * 128 + 128, :])
                + dot(g_ref[m + 32 : m + 384, :], w_ref[384 + b * 128 : 512 + b * 128, :])
                + dot(g_ref[m : m + 352, :], w_ref[768 + b * 128 : 896 + b * 128, :])
            )
    for m in range(0, 1024, 64):
        total[m : m + 64, :] = (
            z[0, m + 2 : m + 66, :] + z[1, m + 1 : m + 65, :] + z[2, m : m + 64, :]
        )
    own_ref[...] = total[pl.ds(pl.multiple_of(core * 512, 512), 512), :]
    send_ref[...] = total[pl.ds(pl.multiple_of((1 - core) * 512, 512), 512), :].astype(BF)


def repack_kernel(own_ref, recv_ref, out_ref):
    parts = []
    for hh in range(2):
        rows = []
        for hl in range(8):
            at = (hh * 8 + hl) * 32
            row = own_ref[at : at + 32, :] + recv_ref[at : at + 32, :].astype(F32)
            rows.append(row[0:NCOL])
        parts.append([swap_blocks([r[:, q : q + 128] for r in rows], 16) for q in (0, 128)])
    for d in range(16):
        out_ref[d] = jnp.concatenate(
            [parts[0][d // 8][d % 8], parts[1][d // 8][d % 8]], axis=0
        ).astype(BF)


def restore_kernel(r_ref, out_ref):
    halves = [[], []]
    for j in range(16):
        chunk = r_ref[j].astype(F32)
        halves[0].append(chunk[0:NCOL])
        halves[1].append(chunk[NCOL : 2 * NCOL])
    field = jnp.concatenate(
        [jnp.concatenate(half, axis=0) for half in halves], axis=1
    ).astype(BF)
    row = iota((256, 256), 0)
    pick = iota((256, 256), 1) == (row & 15) * 16 + (row >> 4)
    out = dot(jnp.where(pick, 1.0, 0.0).astype(BF), field, NT)
    out_ref[...] = out.astype(BF).reshape(16, 16, 384)


def sum_kernel(r_ref, out_ref):
    total = r_ref[0].astype(F32)
    for s in range(1, 128):
        total = total + r_ref[s].astype(F32)
    for b in range(16):
        out_ref[b] = total


def order_kernel(r_ref, out_ref):
    for m in range(8):
        for core in range(2):
            for ih in range(2):
                out_ref[m, 8 * core : 8 * core + 8, 128 * ih : 128 * ih + 128] = r_ref[
                    2 * m + core, 8 * ih : 8 * ih + 8, :
                ]
    for core in range(2):
        for ih in range(2):
            out_ref[8, 8 * core : 8 * core + 8, 128 * ih : 128 * ih + 128] = r_ref[
                8 * ih + core, 16:24, :
            ]


def shards(inputs, cotangent, kernel, channel_bias):
    core = lax.axis_index("core").astype(jnp.int32).reshape(1)
    taps = kernel.reshape(16, 9, 256).transpose(1, 0, 2)
    (packed,) = call(
        pack_kernel,
        [((16, 272, 128), BF)],
        core,
        inputs,
        cotangent,
        taps,
        channel_bias.reshape(1, 16),
    )
    got = lax.all_to_all(packed, CHAN, 0, 0)
    xo, co, ha, hb, w = call(
        unpack_kernel,
        [((768, 256), BF), ((512, 128), BF), ((96, 256), BF), ((96, 256), BF), ((1152, 256), BF)],
        core,
        got,
    )
    across = [(b, b + 1) for b in range(1, 15, 2)]
    across += [(b + 1, b) for b in range(1, 15, 2)]
    along = [(b, b + 2) for b in range(1, 14, 2)] + [(b, b - 2) for b in range(2, 16, 2)]
    xr = lax.ppermute(xo, "core", [(0, 1), (1, 0)])
    ha = lax.ppermute(ha, BAND, across)
    hb = lax.ppermute(hb, BAND, along)
    scale = 1.0 / math.sqrt(256 * 384)

    def grads(*refs):
        grad_kernel(scale, *refs)

    kg, g = call(
        grads,
        [((128, 24, 128), BF), ((PX, 128), BF)],
        core,
        xo,
        xr,
        co,
        ha,
        hb,
        w,
        scratch=[
            pltpu.VMEM((1216, 256), BF),
            pltpu.VMEM((1088, 128), BF),
            pltpu.VMEM((PX, 384), F32),
            pltpu.VMEM((PX + 16, 128), F32),
        ],
    )
    kg = lax.all_to_all(kg, ("xl", "y", "z", "xh"), 0, 0)
    own, send = call(
        input_kernel,
        [((512, 256), F32), ((512, 256), BF)],
        core,
        g,
        w,
        scratch=[pltpu.VMEM((3, 1056, 256), F32), pltpu.VMEM((1024, 256), F32)],
    )
    recv = lax.ppermute(send, "core", [(0, 1), (1, 0)])
    (back,) = call(repack_kernel, [((16, 48, 128), BF)], own, recv, smem=False)
    back = lax.all_to_all(back, CHAN, 0, 0)
    (input_grad,) = call(restore_kernel, [((16, 16, 384), BF)], back, smem=False)
    (pieces,) = call(sum_kernel, [((16, 24, 128), F32)], kg, smem=False)
    pieces = lax.all_to_all(pieces, BAND, 0, 0)
    (ordered,) = call(order_kernel, [((9, 16, 256), F32)], pieces, smem=False)
    kernel_grad = ordered.transpose(1, 0, 2).reshape(16, 3, 3, 256)
    return (input_grad, kernel_grad)


def solution(mesh):
    fine = Mesh(mesh.devices.reshape(2, 4, 2, 8, 2), ("xl", "y", "core", "z", "xh"))
    return jax.shard_map(
        shards,
        mesh=fine,
        in_specs=(
            P(CHAN, BAND, None),
            P(CHAN, BAND, None),
            P(CHAN, None, None, None),
            P(CHAN),
        ),
        out_specs=(P(CHAN, BAND, None), P(CHAN, None, None, None)),
        check_vma=False,
    )
```

```python
import math

import jax
import jax.numpy as jnp
from jax import lax
from jax.experimental import pallas as pl
from jax.experimental.pallas import tpu as pltpu
from jax.sharding import Mesh
from jax.sharding import PartitionSpec as P

BF = jnp.bfloat16
F32 = jnp.float32
CHAN = ("z", "xh")
BAND = ("xl", "y", "core")
PITCH = 32
NCOL = 24
PX = 1152
NT = (((1,), (1,)), ((), ()))
TN = (((0,), (0,)), ((), ()))


def dot(a, b, dims=(((1,), (0,)), ((), ()))):
    return lax.dot_general(a, b, dims, preferred_element_type=F32)


def iota(shape, dim):
    return lax.broadcasted_iota(jnp.int32, shape, dim)


def call(body, outs, *args, smem=True, scratch=(), hbm=(), mib=48):
    specs = [
        pl.BlockSpec(memory_space=pltpu.HBM if k in hbm else pltpu.VMEM) for k in range(len(args))
    ]
    if smem:
        specs[0] = pl.BlockSpec(memory_space=pltpu.SMEM)
    return pl.pallas_call(
        body,
        out_shape=[jax.ShapeDtypeStruct(s, d) for s, d in outs],
        in_specs=specs,
        out_specs=[pl.BlockSpec(memory_space=pltpu.VMEM)] * len(outs),
        scratch_shapes=list(scratch),
        compiler_params=pltpu.CompilerParams(vmem_limit_bytes=mib * 1024 * 1024),
    )(*args)


def swap_blocks(arrays, block):
    lanes = arrays[0].shape[1]
    place = iota(arrays[0].shape, 1) // block
    bit = 1
    while bit < len(arrays):
        upper = (place & bit) != 0
        out = list(arrays)
        for s in range(len(arrays)):
            if s & bit:
                continue
            a, b = arrays[s], arrays[s | bit]
            out[s] = jnp.where(upper, pltpu.roll(b, bit * block, 1), a)
            out[s | bit] = jnp.where(upper, b, pltpu.roll(a, lanes - bit * block, 1))
        arrays = out
        bit *= 2
    return arrays


def window(first, count):
    row = iota((512, 384), 0)
    c = row & 31
    hit = (iota((512, 384), 1) == (row >> 5) * NCOL + c + first) & (c < count)
    return jnp.where(hit, 1.0, 0.0).astype(BF)


def pack_kernel(place_ref, *refs):
    out_ref, sems = refs[4], refs[9]
    copies = [pltpu.make_async_copy(refs[k], refs[5 + k], sems.at[k]) for k in range(4)]
    for copy in copies:
        copy.start()
    x_ref, cot_ref, bias_ref, ker_ref = refs[5:9]
    core = place_ref[0]
    src = iota((256, 256), 0)
    dst = iota((256, 256), 1)
    ch, h = src >> 4, src & 15
    to_h_ch = jnp.where(dst == h * 16 + ch, 1.0, 0.0).astype(BF)
    other = (ch >> 3) ^ core
    to_half = jnp.where(dst == other * 128 + h * 8 + (ch & 7), 1.0, 0.0).astype(BF)

    copies[0].wait()
    x = dot(window(-2, 28), x_ref[...].reshape(256, 384), NT).astype(BF)
    x = dot(x, to_h_ch).astype(BF).reshape(16, 32, 256)
    out_ref[:, 0:32, :] = x[:, :, 0:128]
    out_ref[:, 32:64, :] = x[:, :, 128:256]

    copies[2].wait()
    bias = jnp.broadcast_to(bias_ref[...], (8, 16))
    hi = bias.astype(BF).astype(F32)
    mid = (bias - hi).astype(BF).astype(F32)
    low = bias - hi - mid
    k = iota((8, 16), 0)
    pieces = jnp.where(k == 4, hi, jnp.where(k == 5, mid, jnp.where(k == 6, low, 0.0)))
    spread = iota((16, 128), 0) == (core * 8 + (iota((16, 128), 1) & 7))
    pieces = dot(pieces.astype(BF), jnp.where(spread, 1.0, 0.0).astype(BF))
    rows = jnp.concatenate([jnp.zeros((24, 128), F32), pieces], axis=0)

    copies[1].wait()
    c = dot(window(-1, 26), cot_ref[...].reshape(256, 384), NT).astype(BF)
    c = dot(c, to_half).reshape(16, 32, 256)
    out_ref[:, 64:96, :] = (c[:, :, 0:128] + rows[None]).astype(BF)
    out_ref[:, 96:128, :] = c[:, :, 128:256].astype(BF)

    copies[3].wait()
    parts = []
    for t in range(9):
        both = ker_ref[t].astype(F32)
        mine = jnp.where(core == 0, both[0:8], both[8:16])
        parts.append(jnp.where(place_ref[1] == 0, mine[:, 0:128], mine[:, 128:256]))
    parts.append(jnp.zeros((8, 128), F32))
    weights = jnp.concatenate(parts, axis=0).astype(BF)
    for j in range(16):
        out_ref[j, 128:208, :] = weights


SOURCES = [z * 2 + xh for xh in range(2) for z in range(8)]


def unpack_kernel(core_ref, r_ref, xo_ref, co_ref, ha_ref, hb_ref, w_ref):
    core = core_ref[0]
    edge = []
    for hh in range(2):
        halves = []
        for sh in range(2):
            got = [r_ref[sh * 8 + s, hh * 32 : hh * 32 + 32, :] for s in range(8)]
            halves.append(swap_blocks(got, 16))
        for hl in range(8):
            at = (hh * 8 + hl) * 32
            row = jnp.concatenate([halves[0][hl], halves[1][hl]], axis=1)
            xo_ref[at : at + 32, :] = row
            if (hh * 8 + hl) in (0, 1, 14, 15):
                edge.append(row)
    own = swap_blocks([r_ref[s, 64:96, :] for s in SOURCES], 8)
    oth = swap_blocks([r_ref[s, 96:128, :] for s in SOURCES], 8)
    for h in range(16):
        co_ref[h * 32 : h * 32 + 32, :] = own[h]
        at = 512 + (h % 8) * 32
        xo_ref[at : at + 32, (h // 8) * 128 : (h // 8) * 128 + 128] = oth[h]
    first = core == 0
    blank = jnp.zeros((32, 128), BF)
    for ref, cot in ((ha_ref, oth), (hb_ref, own)):
        ref[0:32, :] = jnp.where(first, edge[0], edge[2])
        ref[32:64, :] = jnp.where(first, edge[1], edge[3])
        ref[64:96, 0:128] = jnp.where(first, cot[0], cot[15])
        ref[64:96, 128:256] = blank
    chunks = [r_ref[s, 128:208, :].astype(F32) for s in SOURCES]
    for t in range(9):
        tap = jnp.concatenate([chunk[t * 8 : t * 8 + 8] for chunk in chunks], axis=0)
        w_ref[t * 128 : t * 128 + 128, :] = tap.astype(BF)


def grad_kernel(scale, place_ref, xo_ref, xr_ref, co_ref, ha_ref, hb_ref, wo_ref, wr_ref, *refs):
    kg_ref, g_ref, w_ref, x, cot, y, gs = refs
    core = place_ref[0]
    low = place_ref[1] == 0
    w_ref[:, 0:128] = jnp.where(low, wo_ref[...], wr_ref[...])
    w_ref[:, 128:256] = jnp.where(low, wr_ref[...], wo_ref[...])
    first = core == 0
    mine = pl.multiple_of(core * 512, 512)
    theirs = pl.multiple_of((1 - core) * 512, 512)
    x[0:64, :] = jnp.where(first, ha_ref[0:64, :], hb_ref[0:64, :])
    x[pl.ds(64 + mine, 512), :] = xo_ref[0:512, :]
    x[pl.ds(64 + theirs, 512), :] = xr_ref[0:512, :]
    x[1088:1152, :] = jnp.where(first, hb_ref[0:64, :], ha_ref[0:64, :])
    x[1152:1216, :] = jnp.zeros((64, 256), BF)
    cot[0:32, :] = jnp.where(first, ha_ref[64:96, 0:128], hb_ref[64:96, 0:128])
    cot[pl.ds(32 + mine, 512), :] = co_ref[...]
    cot[pl.ds(32 + theirs, 256), :] = xr_ref[512:768, 0:128]
    cot[pl.ds(32 + theirs + 256, 256), :] = xr_ref[512:768, 128:256]
    cot[1056:1088, :] = jnp.where(first, hb_ref[64:96, 0:128], ha_ref[64:96, 0:128])

    bias = co_ref[16:32, :].astype(F32)
    bias = bias[12:13] + bias[13:14] + bias[14:15]

    for m in range(0, PX, 384):
        y[m : m + 384, :] = (
            dot(x[m : m + 384, :], w_ref[0:384, :], NT)
            + dot(x[m + 32 : m + 416, :], w_ref[384:768, :], NT)
            + dot(x[m + 64 : m + 448, :], w_ref[768:1152, :], NT)
        )

    gs[0:16, :] = jnp.zeros((16, 128), F32)
    for m in range(0, 1088, 64):
        pre = (
            y[m : m + 64, 0:128]
            + y[m + 1 : m + 65, 128:256]
            + y[m + 2 : m + 66, 256:384]
            + bias
        )
        s = 1.0 / (1.0 + jnp.exp(-pre))
        c = iota((64, 128), 0) & 31
        grad = cot[m : m + 64, :].astype(F32) * s * (1.0 + pre * (1.0 - s))
        grad = jnp.where(c < 26, grad, 0.0).astype(BF)
        g_ref[m : m + 64, :] = grad
        p = iota((64, 128), 0) + m
        inner = (c >= 1) & (c <= NCOL) & (p >= 32) & (p < 1056)
        gs[16 + m : 16 + m + 64, :] = jnp.where(inner, grad.astype(F32), 0.0)
    g_ref[1088:PX, :] = jnp.zeros((PX - 1088, 128), BF)
    gs[16 + 1088 : 16 + PX, :] = jnp.zeros((PX - 1088, 128), F32)

    taps = []
    shifted = jnp.concatenate(
        [gs[16 - b : 16 - b + PX, :].astype(BF) for b in range(3)], axis=1
    )
    for a in range(3):
        block = dot(shifted, x[32 * a : 32 * a + PX, :], TN) * scale
        taps += [block[0:128], block[128:256], block[256:384]]
    for k in range(16):
        o = slice(8 * k, 8 * k + 8)
        rows = [tap[o, lane : lane + 128] for tap in taps for lane in (0, 128)]
        kg_ref[SOURCES[k]] = jnp.concatenate(rows, axis=0).astype(BF)


def input_kernel(core_ref, g_ref, w_ref, own_ref, send_ref, z, total):
    core = core_ref[0]
    for m in (0, 352, 704):
        for b in range(3):
            z[b, m : m + 352, :] = (
                dot(g_ref[m + 64 : m + 416, :], w_ref[b * 128 : b * 128 + 128, :])
                + dot(g_ref[m + 32 : m + 384, :], w_ref[384 + b * 128 : 512 + b * 128, :])
                + dot(g_ref[m : m + 352, :], w_ref[768 + b * 128 : 896 + b * 128, :])
            )
    for m in range(0, 1024, 64):
        total[m : m + 64, :] = (
            z[0, m + 2 : m + 66, :] + z[1, m + 1 : m + 65, :] + z[2, m : m + 64, :]
        )
    own_ref[...] = total[pl.ds(pl.multiple_of(core * 512, 512), 512), :]
    send_ref[...] = total[pl.ds(pl.multiple_of((1 - core) * 512, 512), 512), :].astype(BF)


def repack_kernel(own_ref, recv_ref, out_ref):
    parts = []
    for hh in range(2):
        rows = []
        for hl in range(8):
            at = (hh * 8 + hl) * 32
            row = own_ref[at : at + 32, :] + recv_ref[at : at + 32, :].astype(F32)
            rows.append(row[0:NCOL])
        parts.append([swap_blocks([r[:, q : q + 128] for r in rows], 16) for q in (0, 128)])
    for d in range(16):
        out_ref[d] = jnp.concatenate(
            [parts[0][d // 8][d % 8], parts[1][d // 8][d % 8]], axis=0
        ).astype(BF)


def restore_kernel(r_ref, out_ref):
    halves = [[], []]
    for j in range(16):
        chunk = r_ref[j].astype(F32)
        halves[0].append(chunk[0:NCOL])
        halves[1].append(chunk[NCOL : 2 * NCOL])
    field = jnp.concatenate(
        [jnp.concatenate(half, axis=0) for half in halves], axis=1
    ).astype(BF)
    row = iota((256, 256), 0)
    pick = iota((256, 256), 1) == (row & 15) * 16 + (row >> 4)
    out = dot(jnp.where(pick, 1.0, 0.0).astype(BF), field, NT)
    out_ref[...] = out.astype(BF).reshape(16, 16, 384)


def sum_kernel(r_ref, out_ref):
    total = r_ref[0].astype(F32)
    for s in range(1, 16):
        total = total + r_ref[s].astype(F32)
    out_ref[...] = total.astype(BF)


def ring_kernel(own_ref, next_ref, prev_ref, far_ref, out_ref):
    even = own_ref[...].astype(F32) + far_ref[...].astype(F32)
    odd = next_ref[...].astype(F32) + prev_ref[...].astype(F32)
    out_ref[...] = (even + odd).astype(BF)


def order_kernel(core_ref, own_ref, xl_ref, core_own_ref, core_xl_ref, out_ref):
    first = core_ref[0] == 0
    mine = own_ref[...].astype(F32) + xl_ref[...].astype(F32)
    other = core_own_ref[...].astype(F32) + core_xl_ref[...].astype(F32)
    low = jnp.where(first, mine, other)
    high = jnp.where(first, other, mine)
    for t in range(9):
        for ih in range(2):
            rows = slice((t * 2 + ih) * 8, (t * 2 + ih) * 8 + 8)
            out_ref[t, 0:8, ih * 128 : ih * 128 + 128] = low[rows]
            out_ref[t, 8:16, ih * 128 : ih * 128 + 128] = high[rows]


def shards(inputs, cotangent, kernel, channel_bias):
    core, y = (lax.axis_index(n).astype(jnp.int32) for n in ("core", "y"))
    place = jnp.stack([core, y & 1])
    (packed,) = call(
        pack_kernel,
        [((16, 208, 128), BF)],
        place,
        inputs,
        cotangent,
        channel_bias.reshape(1, 16),
        kernel.reshape(16, 9, 256).transpose(1, 0, 2),
        hbm=(1, 2, 3, 4),
        mib=56,
        scratch=[
            pltpu.VMEM((16, 16, 384), BF),
            pltpu.VMEM((16, 16, 384), BF),
            pltpu.VMEM((1, 16), F32),
            pltpu.VMEM((9, 16, 256), BF),
            pltpu.SemaphoreType.DMA((4,)),
        ],
    )
    got = lax.all_to_all(packed, CHAN, 0, 0)
    xo, co, ha, hb, w_here = call(
        unpack_kernel,
        [((768, 256), BF), ((512, 128), BF), ((96, 256), BF), ((96, 256), BF), ((1152, 128), BF)],
        core.reshape(1),
        got,
    )
    w_there = lax.ppermute(w_here, "y", [(i, i ^ 1) for i in range(4)])
    across = [(b, b + 1) for b in range(1, 15, 2)]
    across += [(b + 1, b) for b in range(1, 15, 2)]
    along = [(b, b + 2) for b in range(1, 14, 2)] + [(b, b - 2) for b in range(2, 16, 2)]
    xr = lax.ppermute(xo, "core", [(0, 1), (1, 0)])
    ha = lax.ppermute(ha, BAND, across)
    hb = lax.ppermute(hb, BAND, along)
    scale = 1.0 / math.sqrt(256 * 384)

    def grads(*refs):
        grad_kernel(scale, *refs)

    kg, g, w = call(
        grads,
        [((16, 144, 128), BF), ((PX, 128), BF), ((1152, 256), BF)],
        place,
        xo,
        xr,
        co,
        ha,
        hb,
        w_here,
        w_there,
        scratch=[
            pltpu.VMEM((1216, 256), BF),
            pltpu.VMEM((1088, 128), BF),
            pltpu.VMEM((PX, 384), F32),
            pltpu.VMEM((PX + 16, 128), F32),
        ],
    )
    kg = lax.all_to_all(kg, CHAN, 0, 0)
    own, send = call(
        input_kernel,
        [((512, 256), F32), ((512, 256), BF)],
        core.reshape(1),
        g,
        w,
        scratch=[pltpu.VMEM((3, 1056, 256), F32), pltpu.VMEM((1024, 256), F32)],
    )
    recv = lax.ppermute(send, "core", [(0, 1), (1, 0)])
    (back,) = call(repack_kernel, [((16, 48, 128), BF)], own, recv, smem=False)
    back = lax.all_to_all(back, CHAN, 0, 0)
    (input_grad,) = call(restore_kernel, [((16, 16, 384), BF)], back, smem=False)

    part = ((144, 128), BF)
    (sums,) = call(sum_kernel, [part], kg, smem=False)
    ring = [lax.ppermute(sums, "y", [(i, (i + k) % 4) for i in range(4)]) for k in (3, 1, 2)]
    (sums,) = call(ring_kernel, [part], sums, *ring, smem=False)
    (ordered,) = call(
        order_kernel,
        [((9, 16, 256), F32)],
        core.reshape(1),
        sums,
        lax.ppermute(sums, "xl", [(0, 1), (1, 0)]),
        lax.ppermute(sums, "core", [(0, 1), (1, 0)]),
        lax.ppermute(sums, ("xl", "core"), [(i, i ^ 3) for i in range(4)]),
    )
    kernel_grad = ordered.transpose(1, 0, 2).reshape(16, 3, 3, 256)
    return (input_grad, kernel_grad)


def solution(mesh):
    fine = Mesh(mesh.devices.reshape(2, 4, 2, 8, 2), ("xl", "y", "core", "z", "xh"))
    return jax.shard_map(
        shards,
        mesh=fine,
        in_specs=(
            P(CHAN, BAND, None),
            P(CHAN, BAND, None),
            P(CHAN, None, None, None),
            P(CHAN),
        ),
        out_specs=(P(CHAN, BAND, None), P(CHAN, None, None, None)),
        check_vma=False,
    )
```

```python
import math

import jax
import jax.numpy as jnp
from jax import lax
from jax.experimental import pallas as pl
from jax.experimental.pallas import tpu as pltpu
from jax.sharding import Mesh
from jax.sharding import PartitionSpec as P

BF = jnp.bfloat16
F32 = jnp.float32
CHAN = ("z", "xh")
BAND = ("xl", "y", "core")
PITCH = 32
NCOL = 24
PX = 1152
NT = (((1,), (1,)), ((), ()))
TN = (((0,), (0,)), ((), ()))


def dot(a, b, dims=(((1,), (0,)), ((), ()))):
    return lax.dot_general(a, b, dims, preferred_element_type=F32)


def iota(shape, dim):
    return lax.broadcasted_iota(jnp.int32, shape, dim)


def call(body, outs, *args, smem=1, scratch=(), hbm=(), copied=(), mib=48):
    specs = [
        pl.BlockSpec(
            memory_space=pltpu.SMEM if k < smem else pltpu.HBM if k in hbm else pltpu.VMEM
        )
        for k in range(len(args))
    ]
    return pl.pallas_call(
        body,
        out_shape=[jax.ShapeDtypeStruct(s, d) for s, d in outs],
        in_specs=specs,
        out_specs=[
            pl.BlockSpec(memory_space=pltpu.HBM if k in copied else pltpu.VMEM)
            for k in range(len(outs))
        ],
        scratch_shapes=list(scratch),
        compiler_params=pltpu.CompilerParams(vmem_limit_bytes=mib * 1024 * 1024),
    )(*args)


def swap_blocks(arrays, block):
    lanes = arrays[0].shape[1]
    place = iota(arrays[0].shape, 1) // block
    bit = 1
    while bit < len(arrays):
        upper = (place & bit) != 0
        out = list(arrays)
        for s in range(len(arrays)):
            if s & bit:
                continue
            a, b = arrays[s], arrays[s | bit]
            out[s] = jnp.where(upper, pltpu.roll(b, bit * block, 1), a)
            out[s | bit] = jnp.where(upper, b, pltpu.roll(a, lanes - bit * block, 1))
        arrays = out
        bit *= 2
    return arrays


def window(first, count):
    row = iota((512, 1), 0)
    c = row & 31
    column = jnp.where(c < count, (row >> 5) * NCOL + c + first, -1)
    return jnp.where(iota((512, 384), 1) == column, 1.0, 0.0).astype(BF)


def half_up(tile):
    return pltpu.roll(tile, 4, tile.ndim - 2)


def fold(field):
    low = iota((16, 8, 128), 1) < 4
    rest = jnp.where(low, field[:, 24:32, 0:128], half_up(field[:, 24:32, 128:256]))
    return [field[:, 0:24, 0:128], field[:, 0:24, 128:256], rest]


def unfold(chunk):
    rest = chunk[48:56]
    return [
        jnp.concatenate([chunk[0:24], rest], axis=0).astype(BF),
        jnp.concatenate([chunk[24:48], half_up(rest)], axis=0).astype(BF),
    ]


def copy_rows(buffer, out, first, last, sem):
    rows = pl.ds(first, last - first)
    copy = pltpu.make_async_copy(buffer.at[:, rows, :], out.at[:, rows, :], sem)
    copy.start()
    return copy


def pack_kernel(core_ref, y_ref, *refs):
    out_hbm, buffer, sems, out_sems = refs[4], refs[9], refs[10], refs[11]
    copies = [pltpu.make_async_copy(refs[k], refs[5 + k], sems.at[k]) for k in range(4)]
    for copy in copies:
        copy.start()
    ker_ref, bias_ref, x_ref, cot_ref = refs[5:9]
    core = core_ref[0]
    dst = iota((256, 256), 0)
    src = iota((256, 256), 1)
    ch, h = src >> 4, src & 15
    to_h_ch = jnp.where(dst == h * 16 + ch, 1.0, 0.0).astype(BF)
    other = (ch >> 3) ^ core
    to_half = jnp.where(dst == other * 128 + h * 8 + (ch & 7), 1.0, 0.0).astype(BF)
    x_window = window(-2, 28)
    cot_window = window(-1, 26)

    copies[0].wait()
    parts = []
    for t in range(9):
        both = ker_ref[t].astype(F32)
        mine = jnp.where(core == 0, both[0:8], both[8:16])
        parts.append(jnp.where(y_ref[0] == 0, mine[:, 0:128], mine[:, 128:256]))
    parts.append(jnp.zeros((8, 128), F32))
    weights = jnp.concatenate(parts, axis=0).astype(BF)
    for j in range(16):
        buffer[j, 112:192, :] = weights
    sent = [copy_rows(buffer, out_hbm, 112, 192, out_sems.at[0])]

    copies[1].wait()
    bias = jnp.broadcast_to(bias_ref[...], (8, 16))
    hi = bias.astype(BF).astype(F32)
    mid = (bias - hi).astype(BF).astype(F32)
    low = bias - hi - mid
    k = iota((8, 16), 0)
    pieces = jnp.where(k == 2, hi, jnp.where(k == 3, mid, jnp.where(k == 6, low, 0.0)))
    spread = iota((16, 128), 0) == (core * 8 + (iota((16, 128), 1) & 7))
    pieces = dot(pieces.astype(BF), jnp.where(spread, 1.0, 0.0).astype(BF))

    copies[2].wait()
    x = dot(to_h_ch, x_ref[...].reshape(256, 384)).astype(BF)
    x = fold(dot(x_window, x, NT).reshape(16, 32, 256))
    buffer[:, 0:48, :] = jnp.concatenate(x[:2], axis=1).astype(BF)
    sent.append(copy_rows(buffer, out_hbm, 0, 48, out_sems.at[1]))

    copies[3].wait()
    c = dot(to_half, cot_ref[...].reshape(256, 384)).astype(BF)
    c = fold(dot(cot_window, c, NT).reshape(16, 32, 256))
    c[2] = c[2] + pieces[None]
    buffer[:, 48:112, :] = jnp.concatenate([x[2]] + c, axis=1).astype(BF)
    sent.append(copy_rows(buffer, out_hbm, 48, 112, out_sems.at[2]))
    for copy in sent:
        copy.wait()


SOURCES = [z * 2 + xh for xh in range(2) for z in range(8)]


def unpack_kernel(core_ref, r_ref, xo_ref, co_ref, ha_ref, hb_ref):
    core = core_ref[0]
    edge = []
    chunks = [r_ref[s, 0:112, :].astype(F32) for s in range(16)]
    fields = [unfold(chunk[0:56]) for chunk in chunks]
    for hh in range(2):
        halves = []
        for sh in range(2):
            halves.append(swap_blocks([fields[sh * 8 + s][hh] for s in range(8)], 16))
        for hl in range(8):
            at = (hh * 8 + hl) * 32
            row = jnp.concatenate([halves[0][hl], halves[1][hl]], axis=1)
            xo_ref[at : at + 32, :] = row
            if (hh * 8 + hl) in (0, 1, 14, 15):
                edge.append(row)
    cots = [unfold(chunks[s][56:112]) for s in SOURCES]
    own = swap_blocks([cot[0] for cot in cots], 8)
    oth = swap_blocks([cot[1] for cot in cots], 8)
    for h in range(16):
        co_ref[h * 32 : h * 32 + 32, :] = own[h]
        at = 512 + (h % 8) * 32
        xo_ref[at : at + 32, (h // 8) * 128 : (h // 8) * 128 + 128] = oth[h]
    first = core == 0
    blank = jnp.zeros((32, 128), BF)
    for ref, cot in ((ha_ref, oth), (hb_ref, own)):
        ref[0:32, :] = jnp.where(first, edge[0], edge[2])
        ref[32:64, :] = jnp.where(first, edge[1], edge[3])
        ref[64:96, 0:128] = jnp.where(first, cot[0], cot[15])
        ref[64:96, 128:256] = blank
    for k in range(16):
        at = 96 + (k % 8) * 80
        hb_ref[at : at + 80, (k // 8) * 128 : (k // 8) * 128 + 128] = r_ref[SOURCES[k], 112:192, :]


def weight_kernel(y_ref, own_ref, got_ref, w_ref):
    low = y_ref[0] == 0
    own = own_ref[96:736, :].astype(F32).reshape(8, 80, 256)
    got = got_ref[96:736, :].astype(F32).reshape(8, 80, 256)
    for ih, field in enumerate((jnp.where(low, own, got), jnp.where(low, got, own))):
        for t in range(9):
            for k in range(2):
                tap = field[:, t * 8 : t * 8 + 8, k * 128 : k * 128 + 128].reshape(64, 128)
                at = t * 128 + k * 64
                w_ref[at : at + 64, ih * 128 : ih * 128 + 128] = tap.astype(BF)


def grad_kernel(scale, core_ref, edge_ref, xo_ref, xr_ref, co_ref, ha_ref, hb_ref, w_ref, *refs):
    kg_hbm, g_ref, x, cot, y, gs, buffer, sems = refs
    core = core_ref[0]
    first = core == 0
    mine = pl.multiple_of(core * 512, 512)
    theirs = pl.multiple_of((1 - core) * 512, 512)
    keep = edge_ref[0] == 0
    hb_x = jnp.where(keep, hb_ref[0:64, :], jnp.zeros((64, 256), BF))
    hb_c = jnp.where(keep, hb_ref[64:96, 0:128], jnp.zeros((32, 128), BF))
    x[0:64, :] = jnp.where(first, ha_ref[0:64, :], hb_x)
    x[pl.ds(64 + mine, 512), :] = xo_ref[0:512, :]
    x[pl.ds(64 + theirs, 512), :] = xr_ref[0:512, :]
    x[1088:1152, :] = jnp.where(first, hb_x, ha_ref[0:64, :])
    x[1152:1216, :] = jnp.zeros((64, 256), BF)
    cot[0:32, :] = jnp.where(first, ha_ref[64:96, 0:128], hb_c)
    cot[pl.ds(32 + mine, 512), :] = co_ref[...]
    cot[pl.ds(32 + theirs, 256), :] = xr_ref[512:768, 0:128]
    cot[pl.ds(32 + theirs + 256, 256), :] = xr_ref[512:768, 128:256]
    cot[1056:1088, :] = jnp.where(first, hb_c, ha_ref[64:96, 0:128])

    bias = co_ref[16:32, :].astype(F32)
    bias = bias[10:11] + bias[11:12] + bias[14:15]

    for m in range(0, PX, 384):
        y[m : m + 384, :] = (
            dot(x[m : m + 384, :], w_ref[0:384, :], NT)
            + dot(x[m + 32 : m + 416, :], w_ref[384:768, :], NT)
            + dot(x[m + 64 : m + 448, :], w_ref[768:1152, :], NT)
        )

    gs[0:16, :] = jnp.zeros((16, 128), F32)
    for m in range(0, 1088, 64):
        pre = (
            y[m : m + 64, 0:128]
            + y[m + 1 : m + 65, 128:256]
            + y[m + 2 : m + 66, 256:384]
            + bias
        )
        s = 1.0 / (1.0 + jnp.exp(-pre))
        c = iota((64, 128), 0) & 31
        grad = cot[m : m + 64, :].astype(F32) * s * (1.0 + pre * (1.0 - s))
        grad = jnp.where(c < 26, grad, 0.0).astype(BF)
        g_ref[m : m + 64, :] = grad
        p = iota((64, 128), 0) + m
        inner = (c >= 1) & (c <= NCOL) & (p >= 32) & (p < 1056)
        gs[16 + m : 16 + m + 64, :] = jnp.where(inner, grad.astype(F32), 0.0)
    g_ref[1088:PX, :] = jnp.zeros((PX - 1088, 128), BF)
    gs[16 + 1088 : 16 + PX, :] = jnp.zeros((PX - 1088, 128), F32)

    shifted = jnp.concatenate(
        [gs[16 - b : 16 - b + PX, :].astype(BF) for b in range(3)], axis=1
    )
    sent = []
    for a in range(3):
        block = dot(shifted, x[32 * a : 32 * a + PX, :], TN) * scale
        for k in range(16):
            rows = []
            for b in range(3):
                tap = block[128 * b + 8 * k : 128 * b + 8 * k + 8]
                rows += [tap[:, 0:128], tap[:, 128:256]]
            buffer[SOURCES[k], 48 * a : 48 * a + 48, :] = jnp.concatenate(rows, axis=0).astype(BF)
        sent.append(copy_rows(buffer, kg_hbm, 48 * a, 48 * a + 48, sems.at[a]))
    for copy in sent:
        copy.wait()


def input_kernel(core_ref, g_ref, w_ref, own_ref, send_ref, z, total):
    core = core_ref[0]
    for m in (0, 352, 704):
        for b in range(3):
            z[b, m : m + 352, :] = (
                dot(g_ref[m + 64 : m + 416, :], w_ref[b * 128 : b * 128 + 128, :])
                + dot(g_ref[m + 32 : m + 384, :], w_ref[384 + b * 128 : 512 + b * 128, :])
                + dot(g_ref[m : m + 352, :], w_ref[768 + b * 128 : 896 + b * 128, :])
            )
    for m in range(0, 1024, 64):
        total[m : m + 64, :] = (
            z[0, m + 2 : m + 66, :] + z[1, m + 1 : m + 65, :] + z[2, m : m + 64, :]
        )
    own_ref[...] = total[pl.ds(pl.multiple_of(core * 512, 512), 512), :]
    send_ref[...] = total[pl.ds(pl.multiple_of((1 - core) * 512, 512), 512), :].astype(BF)


def repack_kernel(own_ref, recv_ref, out_ref):
    parts = []
    for hh in range(2):
        rows = []
        for hl in range(8):
            at = (hh * 8 + hl) * 32
            row = own_ref[at : at + 32, :] + recv_ref[at : at + 32, :].astype(F32)
            rows.append(row[0:NCOL])
        parts.append([swap_blocks([r[:, q : q + 128] for r in rows], 16) for q in (0, 128)])
    for d in range(16):
        out_ref[d] = jnp.concatenate(
            [parts[0][d // 8][d % 8], parts[1][d // 8][d % 8]], axis=0
        ).astype(BF)


def restore_kernel(r_ref, out_ref):
    halves = [[], []]
    for j in range(16):
        chunk = r_ref[j].astype(F32)
        halves[0].append(chunk[0:NCOL])
        halves[1].append(chunk[NCOL : 2 * NCOL])
    field = jnp.concatenate(
        [jnp.concatenate(half, axis=0) for half in halves], axis=1
    ).astype(BF)
    row = iota((256, 256), 0)
    pick = iota((256, 256), 1) == (row & 15) * 16 + (row >> 4)
    out = dot(jnp.where(pick, 1.0, 0.0).astype(BF), field, NT)
    out_ref[...] = out.astype(BF).reshape(16, 16, 384)


def sum_kernel(r_ref, out_ref):
    total = r_ref[0].astype(F32)
    for s in range(1, 16):
        total = total + r_ref[s].astype(F32)
    out_ref[...] = total.astype(BF)


def ring_kernel(own_ref, next_ref, prev_ref, far_ref, out_ref):
    even = own_ref[...].astype(F32) + far_ref[...].astype(F32)
    odd = next_ref[...].astype(F32) + prev_ref[...].astype(F32)
    out_ref[...] = (even + odd).astype(BF)


def order_kernel(core_ref, own_ref, xl_ref, core_own_ref, core_xl_ref, out_ref):
    first = core_ref[0] == 0
    mine = own_ref[...].astype(F32) + xl_ref[...].astype(F32)
    other = core_own_ref[...].astype(F32) + core_xl_ref[...].astype(F32)
    low = jnp.where(first, mine, other)
    high = jnp.where(first, other, mine)
    for t in range(9):
        for ih in range(2):
            rows = slice((t * 2 + ih) * 8, (t * 2 + ih) * 8 + 8)
            out_ref[t, 0:8, ih * 128 : ih * 128 + 128] = low[rows]
            out_ref[t, 8:16, ih * 128 : ih * 128 + 128] = high[rows]


def shards(inputs, cotangent, kernel, channel_bias):
    core, y, xl = (
        lax.axis_index(n).astype(jnp.int32).reshape(1) for n in ("core", "y", "xl")
    )
    edge = jnp.where(4 * xl + y == 7 * (1 - core), 1, 0).astype(jnp.int32)
    y = y & 1
    (packed,) = call(
        pack_kernel,
        [((16, 192, 128), BF)],
        core,
        y,
        kernel.reshape(16, 9, 256).transpose(1, 0, 2),
        channel_bias.reshape(1, 16),
        inputs,
        cotangent,
        smem=2,
        hbm=(2, 3, 4, 5),
        copied=(0,),
        mib=56,
        scratch=[
            pltpu.VMEM((9, 16, 256), BF),
            pltpu.VMEM((1, 16), F32),
            pltpu.VMEM((16, 16, 384), BF),
            pltpu.VMEM((16, 16, 384), BF),
            pltpu.VMEM((16, 192, 128), BF),
            pltpu.SemaphoreType.DMA((4,)),
            pltpu.SemaphoreType.DMA((3,)),
        ],
    )
    got = lax.all_to_all(packed, CHAN, 0, 0)
    xo, co, ha, hb = call(
        unpack_kernel,
        [((768, 256), BF), ((512, 128), BF), ((96, 256), BF), ((736, 256), BF)],
        core,
        got,
    )
    across = [(b, b + 1) for b in range(1, 15, 2)]
    across += [(b + 1, b) for b in range(1, 15, 2)]
    along = [(b, (b + 2) % 16) for b in range(1, 16, 2)]
    along += [(b, (b - 2) % 16) for b in range(0, 16, 2)]
    xr = lax.ppermute(xo, "core", [(0, 1), (1, 0)])
    ha = lax.ppermute(ha, BAND, across)
    hr = lax.ppermute(hb, BAND, along)
    (w,) = call(weight_kernel, [((1152, 256), BF)], y, hb, hr)
    scale = 1.0 / math.sqrt(256 * 384)

    def grads(*refs):
        grad_kernel(scale, *refs)

    kg, g = call(
        grads,
        [((16, 144, 128), BF), ((PX, 128), BF)],
        core,
        edge,
        xo,
        xr,
        co,
        ha,
        hr,
        w,
        smem=2,
        scratch=[
            pltpu.VMEM((1216, 256), BF),
            pltpu.VMEM((1088, 128), BF),
            pltpu.VMEM((PX, 384), F32),
            pltpu.VMEM((PX + 16, 128), F32),
            pltpu.VMEM((16, 144, 128), BF),
            pltpu.SemaphoreType.DMA((3,)),
        ],
        copied=(0,),
    )
    kg = lax.all_to_all(kg, CHAN, 0, 0)
    own, send = call(
        input_kernel,
        [((512, 256), F32), ((512, 256), BF)],
        core,
        g,
        w,
        scratch=[pltpu.VMEM((3, 1056, 256), F32), pltpu.VMEM((1024, 256), F32)],
    )
    recv = lax.ppermute(send, "core", [(0, 1), (1, 0)])
    (back,) = call(repack_kernel, [((16, 48, 128), BF)], own, recv, smem=0)
    back = lax.all_to_all(back, CHAN, 0, 0)
    (input_grad,) = call(restore_kernel, [((16, 16, 384), BF)], back, smem=0)

    part = ((144, 128), BF)
    (sums,) = call(sum_kernel, [part], kg, smem=0)
    ring = [lax.ppermute(sums, "y", [(i, (i + k) % 4) for i in range(4)]) for k in (3, 1, 2)]
    (sums,) = call(ring_kernel, [part], sums, *ring, smem=0)
    (ordered,) = call(
        order_kernel,
        [((9, 16, 256), F32)],
        core,
        sums,
        lax.ppermute(sums, "xl", [(0, 1), (1, 0)]),
        lax.ppermute(sums, "core", [(0, 1), (1, 0)]),
        lax.ppermute(sums, ("xl", "core"), [(i, i ^ 3) for i in range(4)]),
    )
    kernel_grad = ordered.transpose(1, 0, 2).reshape(16, 3, 3, 256)
    return (input_grad, kernel_grad)


def solution(mesh):
    fine = Mesh(mesh.devices.reshape(2, 4, 2, 8, 2), ("xl", "y", "core", "z", "xh"))
    return jax.shard_map(
        shards,
        mesh=fine,
        in_specs=(
            P(CHAN, BAND, None),
            P(CHAN, BAND, None),
            P(CHAN, None, None, None),
            P(CHAN),
        ),
        out_specs=(P(CHAN, BAND, None), P(CHAN, None, None, None)),
        check_vma=False,
    )
```

```python
import math

import jax
import jax.numpy as jnp
from jax import lax
from jax.experimental import pallas as pl
from jax.experimental.pallas import tpu as pltpu
from jax.sharding import Mesh
from jax.sharding import PartitionSpec as P

BF = jnp.bfloat16
F32 = jnp.float32
CHAN = ("z", "xh")
BAND = ("xl", "y", "core")
PITCH = 32
NCOL = 24
PX = 1152
NT = (((1,), (1,)), ((), ()))
TN = (((0,), (0,)), ((), ()))


def dot(a, b, dims=(((1,), (0,)), ((), ()))):
    return lax.dot_general(a, b, dims, preferred_element_type=F32)


def iota(shape, dim):
    return lax.broadcasted_iota(jnp.int32, shape, dim)


def call(body, outs, *args, smem=1, scratch=(), hbm=(), copied=(), mib=48):
    specs = [
        pl.BlockSpec(
            memory_space=pltpu.SMEM if k < smem else pltpu.HBM if k in hbm else pltpu.VMEM
        )
        for k in range(len(args))
    ]
    return pl.pallas_call(
        body,
        out_shape=[jax.ShapeDtypeStruct(s, d) for s, d in outs],
        in_specs=specs,
        out_specs=[
            pl.BlockSpec(memory_space=pltpu.HBM if k in copied else pltpu.VMEM)
            for k in range(len(outs))
        ],
        scratch_shapes=list(scratch),
        compiler_params=pltpu.CompilerParams(vmem_limit_bytes=mib * 1024 * 1024),
    )(*args)


def swap_blocks(arrays, block):
    lanes = arrays[0].shape[1]
    place = iota(arrays[0].shape, 1) // block
    bit = 1
    while bit < len(arrays):
        upper = (place & bit) != 0
        out = list(arrays)
        for s in range(len(arrays)):
            if s & bit:
                continue
            a, b = arrays[s], arrays[s | bit]
            out[s] = jnp.where(upper, pltpu.roll(b, bit * block, 1), a)
            out[s | bit] = jnp.where(upper, b, pltpu.roll(a, lanes - bit * block, 1))
        arrays = out
        bit *= 2
    return arrays


def window(first, count):
    row = iota((512, 1), 0)
    c = row & 31
    column = jnp.where(c < count, (row >> 5) * NCOL + c + first, -1)
    return jnp.where(iota((512, 384), 1) == column, 1.0, 0.0).astype(BF)


def half_up(tile):
    return pltpu.roll(tile, 4, tile.ndim - 2)


def fold(field):
    low = iota((16, 8, 128), 1) < 4
    rest = jnp.where(low, field[:, 24:32, 0:128], half_up(field[:, 24:32, 128:256]))
    return [field[:, 0:24, 0:128], field[:, 0:24, 128:256], rest]


def unfold(chunk):
    rest = chunk[48:56]
    return [
        jnp.concatenate([chunk[0:24], rest], axis=0).astype(BF),
        jnp.concatenate([chunk[24:48], half_up(rest)], axis=0).astype(BF),
    ]


def copy_rows(buffer, out, first, last, sem):
    rows = pl.ds(first, last - first)
    copy = pltpu.make_async_copy(buffer.at[:, rows, :], out.at[:, rows, :], sem)
    copy.start()
    return copy


def pack_kernel(core_ref, *refs):
    out_hbm, buffer, sems, out_sems = refs[4], refs[9], refs[10], refs[11]
    copies = [pltpu.make_async_copy(refs[k], refs[5 + k], sems.at[k]) for k in range(4)]
    for copy in copies:
        copy.start()
    ker_ref, bias_ref, x_ref, cot_ref = refs[5:9]
    core = core_ref[0]
    dst = iota((256, 256), 0)
    src = iota((256, 256), 1)
    ch, h = src >> 4, src & 15
    to_h_ch = jnp.where(dst == h * 16 + ch, 1.0, 0.0).astype(BF)
    other = (ch >> 3) ^ core
    to_half = jnp.where(dst == other * 128 + h * 8 + (ch & 7), 1.0, 0.0).astype(BF)
    x_window = window(-2, 28)
    cot_window = window(-1, 26)

    copies[0].wait()
    taps = []
    for t in range(9):
        both = ker_ref[t].astype(F32)
        taps.append(jnp.where(core == 0, both[0:8], both[8:16]))
    taps = jnp.concatenate(taps, axis=0).astype(BF)
    for j in range(16):
        lane = (j // 2 % 2) * 128
        buffer[j, 112:184, :] = taps[:, lane : lane + 128]
    sent = [copy_rows(buffer, out_hbm, 112, 184, out_sems.at[0])]

    copies[1].wait()
    bias = jnp.broadcast_to(bias_ref[...], (8, 16))
    hi = bias.astype(BF).astype(F32)
    mid = (bias - hi).astype(BF).astype(F32)
    low = bias - hi - mid
    k = iota((8, 16), 0)
    pieces = jnp.where(k == 2, hi, jnp.where(k == 3, mid, jnp.where(k == 6, low, 0.0)))
    spread = iota((16, 128), 0) == (core * 8 + (iota((16, 128), 1) & 7))
    pieces = dot(pieces.astype(BF), jnp.where(spread, 1.0, 0.0).astype(BF))

    copies[2].wait()
    copies[3].wait()
    x = dot(to_h_ch, x_ref[...].reshape(256, 384)).astype(BF)
    x = fold(dot(x_window, x, NT).reshape(16, 32, 256))
    buffer[:, 0:48, :] = jnp.concatenate(x[:2], axis=1).astype(BF)
    sent.append(copy_rows(buffer, out_hbm, 0, 48, out_sems.at[1]))

    c = dot(to_half, cot_ref[...].reshape(256, 384)).astype(BF)
    c = fold(dot(cot_window, c, NT).reshape(16, 32, 256))
    c[2] = c[2] + pieces[None]
    buffer[:, 48:112, :] = jnp.concatenate([x[2]] + c, axis=1).astype(BF)
    sent.append(copy_rows(buffer, out_hbm, 48, 112, out_sems.at[2]))
    for copy in sent:
        copy.wait()


SOURCES = [z * 2 + xh for xh in range(2) for z in range(8)]


def unpack_kernel(core_ref, r_ref, xo_ref, co_ref, ha_ref, w_ref):
    core = core_ref[0]
    edge = []
    chunks = [r_ref[s, 0:112, :].astype(F32) for s in range(16)]
    fields = [unfold(chunk[0:56]) for chunk in chunks]
    for hh in range(2):
        halves = []
        for sh in range(2):
            halves.append(swap_blocks([fields[sh * 8 + s][hh] for s in range(8)], 16))
        for hl in range(8):
            at = (hh * 8 + hl) * 32
            row = jnp.concatenate([halves[0][hl], halves[1][hl]], axis=1)
            xo_ref[at : at + 32, :] = row
            if (hh * 8 + hl) in (0, 1, 14, 15):
                edge.append(row)
    cots = [unfold(chunks[s][56:112]) for s in SOURCES]
    own = swap_blocks([cot[0] for cot in cots], 8)
    oth = swap_blocks([cot[1] for cot in cots], 8)
    for h in range(16):
        co_ref[h * 32 : h * 32 + 32, :] = own[h]
        at = 512 + (h % 8) * 32
        xo_ref[at : at + 32, (h // 8) * 128 : (h // 8) * 128 + 128] = oth[h]
    first = core == 0
    ha_ref[0:32, :] = jnp.where(first, edge[0], edge[2])
    ha_ref[32:64, :] = jnp.where(first, edge[1], edge[3])
    ha_ref[64:96, 0:128] = jnp.where(first, oth[0], oth[15])
    ha_ref[64:96, 128:256] = jnp.where(first, own[0], own[15])
    for k in range(16):
        w_ref[k] = r_ref[SOURCES[k], 112:184, :]


def weight_kernel(half_ref, own_ref, got_ref, w_ref):
    low = half_ref[0] == 0
    own = own_ref[...].astype(F32)
    got = got_ref[...].astype(F32)
    for ih, field in enumerate((jnp.where(low, own, got), jnp.where(low, got, own))):
        for t in range(9):
            tap = field[:, t * 8 : t * 8 + 8].reshape(128, 128)
            w_ref[t * 128 : t * 128 + 128, ih * 128 : ih * 128 + 128] = tap.astype(BF)


def grad_kernel(scale, core_ref, xo_ref, xr_ref, co_ref, ha_ref, hb_ref, w_ref, *refs):
    kg_hbm, g_ref, x, cot, y, gs, buffer, sems = refs
    core = core_ref[0]
    first = core == 0
    mine = pl.multiple_of(core * 512, 512)
    theirs = pl.multiple_of((1 - core) * 512, 512)
    x[0:64, :] = jnp.where(first, ha_ref[0:64, :], hb_ref[0:64, :])
    x[pl.ds(64 + mine, 512), :] = xo_ref[0:512, :]
    x[pl.ds(64 + theirs, 512), :] = xr_ref[0:512, :]
    x[1088:1152, :] = jnp.where(first, hb_ref[0:64, :], ha_ref[0:64, :])
    x[1152:1216, :] = jnp.zeros((64, 256), BF)
    cot[0:32, :] = jnp.where(first, ha_ref[64:96, 0:128], hb_ref[64:96, 128:256])
    cot[pl.ds(32 + mine, 512), :] = co_ref[...]
    cot[pl.ds(32 + theirs, 256), :] = xr_ref[512:768, 0:128]
    cot[pl.ds(32 + theirs + 256, 256), :] = xr_ref[512:768, 128:256]
    cot[1056:1088, :] = jnp.where(first, hb_ref[64:96, 128:256], ha_ref[64:96, 0:128])

    bias = co_ref[16:32, :].astype(F32)
    bias = bias[10:11] + bias[11:12] + bias[14:15]

    for m in range(0, PX, 384):
        y[m : m + 384, :] = (
            dot(x[m : m + 384, :], w_ref[0:384, :], NT)
            + dot(x[m + 32 : m + 416, :], w_ref[384:768, :], NT)
            + dot(x[m + 64 : m + 448, :], w_ref[768:1152, :], NT)
        )

    gs[0:16, :] = jnp.zeros((16, 128), F32)
    for m in range(0, 1088, 64):
        pre = (
            y[m : m + 64, 0:128]
            + y[m + 1 : m + 65, 128:256]
            + y[m + 2 : m + 66, 256:384]
            + bias
        )
        s = 1.0 / (1.0 + jnp.exp(-pre))
        c = iota((64, 128), 0) & 31
        grad = cot[m : m + 64, :].astype(F32) * s * (1.0 + pre * (1.0 - s))
        grad = jnp.where(c < 26, grad, 0.0).astype(BF)
        g_ref[m : m + 64, :] = grad
        p = iota((64, 128), 0) + m
        inner = (c >= 1) & (c <= NCOL) & (p >= 32) & (p < 1056)
        gs[16 + m : 16 + m + 64, :] = jnp.where(inner, grad.astype(F32), 0.0)
    g_ref[1088:PX, :] = jnp.zeros((PX - 1088, 128), BF)
    gs[16 + 1088 : 16 + PX, :] = jnp.zeros((PX - 1088, 128), F32)

    shifted = jnp.concatenate(
        [gs[16 - b : 16 - b + PX, :].astype(BF) for b in range(3)], axis=1
    )
    sent = []
    for a in range(3):
        block = dot(shifted, x[32 * a : 32 * a + PX, :], TN) * scale
        for k in range(16):
            rows = []
            for b in range(3):
                tap = block[128 * b + 8 * k : 128 * b + 8 * k + 8]
                rows += [tap[:, 0:128], tap[:, 128:256]]
            buffer[SOURCES[k], 48 * a : 48 * a + 48, :] = jnp.concatenate(rows, axis=0).astype(BF)
        sent.append(copy_rows(buffer, kg_hbm, 48 * a, 48 * a + 48, sems.at[a]))
    for copy in sent:
        copy.wait()


def input_kernel(core_ref, g_ref, w_ref, own_ref, send_ref, z, total):
    core = core_ref[0]
    for m in (0, 352, 704):
        for b in range(3):
            z[b, m : m + 352, :] = (
                dot(g_ref[m + 64 : m + 416, :], w_ref[b * 128 : b * 128 + 128, :])
                + dot(g_ref[m + 32 : m + 384, :], w_ref[384 + b * 128 : 512 + b * 128, :])
                + dot(g_ref[m : m + 352, :], w_ref[768 + b * 128 : 896 + b * 128, :])
            )
    for m in range(0, 1024, 64):
        total[m : m + 64, :] = (
            z[0, m + 2 : m + 66, :] + z[1, m + 1 : m + 65, :] + z[2, m : m + 64, :]
        )
    own_ref[...] = total[pl.ds(pl.multiple_of(core * 512, 512), 512), :]
    send_ref[...] = total[pl.ds(pl.multiple_of((1 - core) * 512, 512), 512), :].astype(BF)


def repack_kernel(xh_ref, own_ref, recv_ref, keep_ref, send_ref, chunks):
    parts = []
    for hh in range(2):
        rows = []
        for hl in range(8):
            at = (hh * 8 + hl) * 32
            row = own_ref[at : at + 32, :] + recv_ref[at : at + 32, :].astype(F32)
            rows.append(row[0:NCOL])
        parts.append([swap_blocks([r[:, q : q + 128] for r in rows], 16) for q in (0, 128)])
    for d in range(16):
        chunks[d // 2, d % 2] = jnp.concatenate(
            [parts[0][d // 8][d % 8], parts[1][d // 8][d % 8]], axis=0
        ).astype(BF)
    keep_ref[...] = chunks[:, pl.ds(xh_ref[0], 1)].reshape(8, 48, 128)
    send_ref[...] = chunks[:, pl.ds(1 - xh_ref[0], 1)].reshape(8, 48, 128)


def join_kernel(xh_ref, keep_ref, recv_ref, out_ref):
    first = xh_ref[0] == 0
    out_ref[:, 0:48, :] = jnp.where(first, keep_ref[...], recv_ref[...])
    out_ref[:, 48:96, :] = jnp.where(first, recv_ref[...], keep_ref[...])


def restore_kernel(r_ref, out_ref):
    halves = [[], []]
    for j in range(16):
        chunk = r_ref[j // 2, (j % 2) * 48 : (j % 2) * 48 + 48, :].astype(F32)
        halves[0].append(chunk[0:NCOL])
        halves[1].append(chunk[NCOL : 2 * NCOL])
    field = jnp.concatenate(
        [jnp.concatenate(half, axis=0) for half in halves], axis=1
    ).astype(BF)
    row = iota((256, 256), 0)
    pick = iota((256, 256), 1) == (row & 15) * 16 + (row >> 4)
    out = dot(jnp.where(pick, 1.0, 0.0).astype(BF), field, NT)
    out_ref[...] = out.astype(BF).reshape(16, 16, 384)


def sum_kernel(r_ref, after_ref, out_ref):
    total = r_ref[0].astype(F32)
    for s in range(1, 16):
        total = total + r_ref[s].astype(F32)
    out_ref[...] = total.astype(BF)


def ring_kernel(own_ref, next_ref, prev_ref, far_ref, out_ref):
    even = own_ref[...].astype(F32) + far_ref[...].astype(F32)
    odd = next_ref[...].astype(F32) + prev_ref[...].astype(F32)
    out_ref[...] = (even + odd).astype(BF)


def order_kernel(core_ref, own_ref, xl_ref, core_own_ref, core_xl_ref, out_ref):
    first = core_ref[0] == 0
    mine = own_ref[...].astype(F32) + xl_ref[...].astype(F32)
    other = core_own_ref[...].astype(F32) + core_xl_ref[...].astype(F32)
    low = jnp.where(first, mine, other)
    high = jnp.where(first, other, mine)
    for t in range(9):
        for ih in range(2):
            rows = slice((t * 2 + ih) * 8, (t * 2 + ih) * 8 + 8)
            out_ref[t, 0:8, ih * 128 : ih * 128 + 128] = low[rows]
            out_ref[t, 8:16, ih * 128 : ih * 128 + 128] = high[rows]


def shards(inputs, cotangent, kernel, channel_bias):
    core, z, xh = (
        lax.axis_index(n).astype(jnp.int32).reshape(1) for n in ("core", "z", "xh")
    )
    half = z & 1
    (packed,) = call(
        pack_kernel,
        [((16, 184, 128), BF)],
        core,
        kernel.reshape(16, 9, 256).transpose(1, 0, 2),
        channel_bias.reshape(1, 16),
        inputs,
        cotangent,
        hbm=(1, 2, 3, 4),
        copied=(0,),
        mib=56,
        scratch=[
            pltpu.VMEM((9, 16, 256), BF),
            pltpu.VMEM((1, 16), F32),
            pltpu.VMEM((16, 16, 384), BF),
            pltpu.VMEM((16, 16, 384), BF),
            pltpu.VMEM((16, 184, 128), BF),
            pltpu.SemaphoreType.DMA((4,)),
            pltpu.SemaphoreType.DMA((3,)),
        ],
    )
    got = lax.all_to_all(packed, CHAN, 0, 0)
    xo, co, ha, w_half = call(
        unpack_kernel,
        [((768, 256), BF), ((512, 128), BF), ((96, 256), BF), ((16, 72, 128), BF)],
        core,
        got,
    )
    across = [(b, b + 1) for b in range(1, 15, 2)]
    across += [(b + 1, b) for b in range(1, 15, 2)]
    xr = lax.ppermute(xo, "core", [(0, 1), (1, 0)])
    ha = lax.ppermute(ha, BAND, across)
    hb = lax.ppermute(ha, "core", [(0, 1), (1, 0)])
    ring = [(i, (i + 7) % 8) for i in range(8)] + [(8 + i, 8 + (i + 1) % 8) for i in range(8)]
    w_rest = lax.ppermute(w_half, ("core", "z"), ring)
    (w,) = call(weight_kernel, [((1152, 256), BF)], half, w_half, w_rest)
    scale = 1.0 / math.sqrt(256 * 384)

    def grads(*refs):
        grad_kernel(scale, *refs)

    kg, g = call(
        grads,
        [((16, 144, 128), BF), ((PX, 128), BF)],
        core,
        xo,
        xr,
        co,
        ha,
        hb,
        w,
        scratch=[
            pltpu.VMEM((1216, 256), BF),
            pltpu.VMEM((1088, 128), BF),
            pltpu.VMEM((PX, 384), F32),
            pltpu.VMEM((PX + 16, 128), F32),
            pltpu.VMEM((16, 144, 128), BF),
            pltpu.SemaphoreType.DMA((3,)),
        ],
        copied=(0,),
    )
    kg = lax.all_to_all(kg, CHAN, 0, 0)
    own, send = call(
        input_kernel,
        [((512, 256), F32), ((512, 256), BF)],
        core,
        g,
        w,
        scratch=[pltpu.VMEM((3, 1056, 256), F32), pltpu.VMEM((1024, 256), F32)],
    )
    recv = lax.ppermute(send, "core", [(0, 1), (1, 0)])
    block = ((8, 48, 128), BF)
    keep, send = call(
        repack_kernel,
        [block, block],
        xh,
        own,
        recv,
        scratch=[pltpu.VMEM((8, 2, 48, 128), BF)],
    )
    recv = lax.ppermute(send, "xh", [(0, 1), (1, 0)])
    (joined,) = call(join_kernel, [((8, 96, 128), BF)], xh, keep, recv)
    back = lax.all_to_all(joined, "z", 0, 0)
    (input_grad,) = call(restore_kernel, [((16, 16, 384), BF)], back, smem=0)

    part = ((144, 128), BF)
    (sums,) = call(sum_kernel, [part], kg, joined, smem=0, hbm=(1,))
    ring = [lax.ppermute(sums, "y", [(i, (i + k) % 4) for i in range(4)]) for k in (3, 1, 2)]
    (sums,) = call(ring_kernel, [part], sums, *ring, smem=0)
    (ordered,) = call(
        order_kernel,
        [((9, 16, 256), F32)],
        core,
        sums,
        lax.ppermute(sums, "xl", [(0, 1), (1, 0)]),
        lax.ppermute(sums, "core", [(0, 1), (1, 0)]),
        lax.ppermute(sums, ("xl", "core"), [(i, i ^ 3) for i in range(4)]),
    )
    kernel_grad = ordered.transpose(1, 0, 2).reshape(16, 3, 3, 256)
    return (input_grad, kernel_grad)


def solution(mesh):
    fine = Mesh(mesh.devices.reshape(2, 4, 2, 8, 2), ("xl", "y", "core", "z", "xh"))
    return jax.shard_map(
        shards,
        mesh=fine,
        in_specs=(
            P(CHAN, BAND, None),
            P(CHAN, BAND, None),
            P(CHAN, None, None, None),
            P(CHAN),
        ),
        out_specs=(P(CHAN, BAND, None), P(CHAN, None, None, None)),
        check_vma=False,
    )
```

```python
import math

import jax
import jax.numpy as jnp
from jax import lax
from jax.experimental import pallas as pl
from jax.experimental.pallas import tpu as pltpu
from jax.sharding import Mesh
from jax.sharding import PartitionSpec as P

BF = jnp.bfloat16
F32 = jnp.float32
CHAN = ("z", "xh")
BAND = ("xl", "y", "core")
PITCH = 32
NCOL = 24
PX = 1152
NT = (((1,), (1,)), ((), ()))
TN = (((0,), (0,)), ((), ()))


def dot(a, b, dims=(((1,), (0,)), ((), ()))):
    return lax.dot_general(a, b, dims, preferred_element_type=F32)


def iota(shape, dim):
    return lax.broadcasted_iota(jnp.int32, shape, dim)


def call(body, outs, *args, smem=1, scratch=(), hbm=(), copied=(), mib=48):
    specs = [
        pl.BlockSpec(
            memory_space=pltpu.SMEM if k < smem else pltpu.HBM if k in hbm else pltpu.VMEM
        )
        for k in range(len(args))
    ]
    return pl.pallas_call(
        body,
        out_shape=[jax.ShapeDtypeStruct(s, d) for s, d in outs],
        in_specs=specs,
        out_specs=[
            pl.BlockSpec(memory_space=pltpu.HBM if k in copied else pltpu.VMEM)
            for k in range(len(outs))
        ],
        scratch_shapes=list(scratch),
        compiler_params=pltpu.CompilerParams(vmem_limit_bytes=mib * 1024 * 1024),
    )(*args)


def swap_blocks(arrays, block):
    lanes = arrays[0].shape[1]
    place = iota(arrays[0].shape, 1) // block
    bit = 1
    while bit < len(arrays):
        upper = (place & bit) != 0
        out = list(arrays)
        for s in range(len(arrays)):
            if s & bit:
                continue
            a, b = arrays[s], arrays[s | bit]
            out[s] = jnp.where(upper, pltpu.roll(b, bit * block, 1), a)
            out[s | bit] = jnp.where(upper, b, pltpu.roll(a, lanes - bit * block, 1))
        arrays = out
        bit *= 2
    return arrays


def window(first, count):
    row = iota((512, 1), 0)
    c = row & 31
    column = jnp.where(c < count, (row >> 5) * NCOL + c + first, -1)
    return jnp.where(iota((512, 384), 1) == column, 1.0, 0.0).astype(BF)


def half_up(tile):
    return pltpu.roll(tile, 4, tile.ndim - 2)


def fold(field):
    low = iota((16, 8, 128), 1) < 4
    rest = jnp.where(low, field[:, 24:32, 0:128], half_up(field[:, 24:32, 128:256]))
    return [field[:, 0:24, 0:128], field[:, 0:24, 128:256], rest]


def unfold(chunk):
    rest = chunk[48:56]
    return [
        jnp.concatenate([chunk[0:24], rest], axis=0).astype(BF),
        jnp.concatenate([chunk[24:48], half_up(rest)], axis=0).astype(BF),
    ]


def copy_rows(buffer, out, first, last, sem):
    rows = pl.ds(first, last - first)
    copy = pltpu.make_async_copy(buffer.at[:, rows, :], out.at[:, rows, :], sem)
    copy.start()
    return copy


def pack_kernel(core_ref, *refs):
    out_hbm, buffer, sems, out_sems = refs[4], refs[9], refs[10], refs[11]
    copies = [pltpu.make_async_copy(refs[k], refs[5 + k], sems.at[k]) for k in range(4)]
    for copy in copies:
        copy.start()
    ker_ref, bias_ref, x_ref, cot_ref = refs[5:9]
    core = core_ref[0]
    dst = iota((256, 256), 0)
    src = iota((256, 256), 1)
    ch, h = src >> 4, src & 15
    to_h_ch = jnp.where(dst == h * 16 + ch, 1.0, 0.0).astype(BF)
    other = (ch >> 3) ^ core
    to_half = jnp.where(dst == other * 128 + h * 8 + (ch & 7), 1.0, 0.0).astype(BF)
    x_window = window(-2, 28)
    cot_window = window(-1, 26)

    copies[0].wait()
    upper = iota((8, 256), 0) < 4
    mine = []
    for t in range(9):
        both = ker_ref[t].astype(F32)
        mine.append(jnp.where(core == 0, both[0:8], both[8:16]))
    halves = []
    for r in range(2):
        taps = [mine[t] if (t % 2 == r) else half_up(mine[t]) for t in range(9)] + [mine[8]]
        pairs = [jnp.where(upper, taps[t], taps[t + 1]) for t in range(0, 10, 2)]
        halves.append(jnp.concatenate(pairs, axis=0).astype(BF))
    for j in range(16):
        lane = (j // 2 % 2) * 128
        buffer[j, 112:152, :] = halves[j // 4 % 2][:, lane : lane + 128]
    sent = [copy_rows(buffer, out_hbm, 112, 152, out_sems.at[0])]

    copies[1].wait()
    bias = jnp.broadcast_to(bias_ref[...], (8, 16))
    hi = bias.astype(BF).astype(F32)
    mid = (bias - hi).astype(BF).astype(F32)
    low = bias - hi - mid
    k = iota((8, 16), 0)
    pieces = jnp.where(k == 2, hi, jnp.where(k == 3, mid, jnp.where(k == 6, low, 0.0)))
    spread = iota((16, 128), 0) == (core * 8 + (iota((16, 128), 1) & 7))
    pieces = dot(pieces.astype(BF), jnp.where(spread, 1.0, 0.0).astype(BF))

    copies[2].wait()
    copies[3].wait()
    x = dot(to_h_ch, x_ref[...].reshape(256, 384)).astype(BF)
    x = fold(dot(x_window, x, NT).reshape(16, 32, 256))
    buffer[:, 0:48, :] = jnp.concatenate(x[:2], axis=1).astype(BF)
    sent.append(copy_rows(buffer, out_hbm, 0, 48, out_sems.at[1]))

    c = dot(to_half, cot_ref[...].reshape(256, 384)).astype(BF)
    c = fold(dot(cot_window, c, NT).reshape(16, 32, 256))
    c[2] = c[2] + pieces[None]
    buffer[:, 48:112, :] = jnp.concatenate([x[2]] + c, axis=1).astype(BF)
    sent.append(copy_rows(buffer, out_hbm, 48, 112, out_sems.at[2]))
    for copy in sent:
        copy.wait()


SOURCES = [z * 2 + xh for xh in range(2) for z in range(8)]


def unpack_kernel(core_ref, r_ref, xo_ref, co_ref, ha_ref, w_ref):
    core = core_ref[0]
    edge = []
    chunks = [r_ref[s, 0:112, :].astype(F32) for s in range(16)]
    fields = [unfold(chunk[0:56]) for chunk in chunks]
    for hh in range(2):
        halves = []
        for sh in range(2):
            halves.append(swap_blocks([fields[sh * 8 + s][hh] for s in range(8)], 16))
        for hl in range(8):
            at = (hh * 8 + hl) * 32
            row = jnp.concatenate([halves[0][hl], halves[1][hl]], axis=1)
            xo_ref[at : at + 32, :] = row
            if (hh * 8 + hl) in (0, 1, 14, 15):
                edge.append(row)
    cots = [unfold(chunks[s][56:112]) for s in SOURCES]
    own = swap_blocks([cot[0] for cot in cots], 8)
    oth = swap_blocks([cot[1] for cot in cots], 8)
    for h in range(16):
        co_ref[h * 32 : h * 32 + 32, :] = own[h]
        at = 512 + (h % 8) * 32
        xo_ref[at : at + 32, (h // 8) * 128 : (h // 8) * 128 + 128] = oth[h]
    first = core == 0
    ha_ref[0:32, :] = jnp.where(first, edge[0], edge[2])
    ha_ref[32:64, :] = jnp.where(first, edge[1], edge[3])
    ha_ref[64:96, 0:128] = jnp.where(first, oth[0], oth[15])
    ha_ref[64:96, 128:256] = jnp.where(first, own[0], own[15])
    for k in range(16):
        w_ref[k] = r_ref[SOURCES[k], 112:152, :]


def weight_kernel(z_ref, own_ref, below_ref, above_ref, far_ref, w_ref, quarters):
    for ref, offset in ((own_ref, 0), (below_ref, 3), (above_ref, 1), (far_ref, 2)):
        quarters[(z_ref[0] + offset) & 3] = ref[...]
    upper = iota((16, 8, 128), 1) < 4
    for ih in range(2):
        first, second = quarters[ih].astype(F32), quarters[2 + ih].astype(F32)
        for t in range(9):
            rows = slice((t // 2) * 8, (t // 2) * 8 + 8)
            if t % 2 == 0:
                tap = jnp.where(upper, first[:, rows], half_up(second[:, rows]))
            else:
                tap = jnp.where(upper, half_up(first[:, rows]), second[:, rows])
            w_ref[t * 128 : t * 128 + 128, ih * 128 : ih * 128 + 128] = tap.reshape(
                128, 128
            ).astype(BF)


def grad_kernel(scale, core_ref, xo_ref, xr_ref, co_ref, ha_ref, hb_ref, w_ref, *refs):
    kg_hbm, g_ref, x, cot, y, gs, buffer, sems = refs
    core = core_ref[0]
    first = core == 0
    mine = pl.multiple_of(core * 512, 512)
    theirs = pl.multiple_of((1 - core) * 512, 512)
    x[0:64, :] = jnp.where(first, ha_ref[0:64, :], hb_ref[0:64, :])
    x[pl.ds(64 + mine, 512), :] = xo_ref[0:512, :]
    x[pl.ds(64 + theirs, 512), :] = xr_ref[0:512, :]
    x[1088:1152, :] = jnp.where(first, hb_ref[0:64, :], ha_ref[0:64, :])
    x[1152:1216, :] = jnp.zeros((64, 256), BF)
    cot[0:32, :] = jnp.where(first, ha_ref[64:96, 0:128], hb_ref[64:96, 128:256])
    cot[pl.ds(32 + mine, 512), :] = co_ref[...]
    cot[pl.ds(32 + theirs, 256), :] = xr_ref[512:768, 0:128]
    cot[pl.ds(32 + theirs + 256, 256), :] = xr_ref[512:768, 128:256]
    cot[1056:1088, :] = jnp.where(first, hb_ref[64:96, 128:256], ha_ref[64:96, 0:128])

    bias = co_ref[16:32, :].astype(F32)
    bias = bias[10:11] + bias[11:12] + bias[14:15]

    for m in range(0, PX, 384):
        y[m : m + 384, :] = (
            dot(x[m : m + 384, :], w_ref[0:384, :], NT)
            + dot(x[m + 32 : m + 416, :], w_ref[384:768, :], NT)
            + dot(x[m + 64 : m + 448, :], w_ref[768:1152, :], NT)
        )

    gs[0:16, :] = jnp.zeros((16, 128), F32)
    for m in range(0, 1088, 64):
        pre = (
            y[m : m + 64, 0:128]
            + y[m + 1 : m + 65, 128:256]
            + y[m + 2 : m + 66, 256:384]
            + bias
        )
        s = 1.0 / (1.0 + jnp.exp(-pre))
        c = iota((64, 128), 0) & 31
        grad = cot[m : m + 64, :].astype(F32) * s * (1.0 + pre * (1.0 - s))
        grad = jnp.where(c < 26, grad, 0.0).astype(BF)
        g_ref[m : m + 64, :] = grad
        p = iota((64, 128), 0) + m
        inner = (c >= 1) & (c <= NCOL) & (p >= 32) & (p < 1056)
        gs[16 + m : 16 + m + 64, :] = jnp.where(inner, grad.astype(F32), 0.0)
    g_ref[1088:PX, :] = jnp.zeros((PX - 1088, 128), BF)
    gs[16 + 1088 : 16 + PX, :] = jnp.zeros((PX - 1088, 128), F32)

    shifted = jnp.concatenate(
        [gs[16 - b : 16 - b + PX, :].astype(BF) for b in range(3)], axis=1
    )
    sent = []
    for a in range(3):
        block = dot(shifted, x[32 * a : 32 * a + PX, :], TN) * scale
        for k in range(16):
            rows = []
            for b in range(3):
                tap = block[128 * b + 8 * k : 128 * b + 8 * k + 8]
                rows += [tap[:, 0:128], tap[:, 128:256]]
            buffer[SOURCES[k], 48 * a : 48 * a + 48, :] = jnp.concatenate(rows, axis=0).astype(BF)
        sent.append(copy_rows(buffer, kg_hbm, 48 * a, 48 * a + 48, sems.at[a]))
    for copy in sent:
        copy.wait()


def input_kernel(core_ref, g_ref, w_ref, own_ref, send_ref, z, total):
    core = core_ref[0]
    for m in (0, 352, 704):
        for b in range(3):
            z[b, m : m + 352, :] = (
                dot(g_ref[m + 64 : m + 416, :], w_ref[b * 128 : b * 128 + 128, :])
                + dot(g_ref[m + 32 : m + 384, :], w_ref[384 + b * 128 : 512 + b * 128, :])
                + dot(g_ref[m : m + 352, :], w_ref[768 + b * 128 : 896 + b * 128, :])
            )
    for m in range(0, 1024, 64):
        total[m : m + 64, :] = (
            z[0, m + 2 : m + 66, :] + z[1, m + 1 : m + 65, :] + z[2, m : m + 64, :]
        )
    own_ref[...] = total[pl.ds(pl.multiple_of(core * 512, 512), 512), :]
    send_ref[...] = total[pl.ds(pl.multiple_of((1 - core) * 512, 512), 512), :].astype(BF)


def repack_kernel(xh_ref, own_ref, recv_ref, keep_ref, send_ref, chunks):
    parts = []
    for hh in range(2):
        rows = []
        for hl in range(8):
            at = (hh * 8 + hl) * 32
            row = own_ref[at : at + 32, :] + recv_ref[at : at + 32, :].astype(F32)
            rows.append(row[0:NCOL])
        parts.append([swap_blocks([r[:, q : q + 128] for r in rows], 16) for q in (0, 128)])
    for d in range(16):
        chunks[d // 2, d % 2] = jnp.concatenate(
            [parts[0][d // 8][d % 8], parts[1][d // 8][d % 8]], axis=0
        ).astype(BF)
    keep_ref[...] = chunks[:, pl.ds(xh_ref[0], 1)].reshape(8, 48, 128)
    send_ref[...] = chunks[:, pl.ds(1 - xh_ref[0], 1)].reshape(8, 48, 128)


def join_kernel(xh_ref, keep_ref, recv_ref, out_ref):
    first = xh_ref[0] == 0
    out_ref[:, 0:48, :] = jnp.where(first, keep_ref[...], recv_ref[...])
    out_ref[:, 48:96, :] = jnp.where(first, recv_ref[...], keep_ref[...])


def restore_kernel(r_ref, out_ref):
    halves = [[], []]
    for j in range(16):
        chunk = r_ref[j // 2, (j % 2) * 48 : (j % 2) * 48 + 48, :].astype(F32)
        halves[0].append(chunk[0:NCOL])
        halves[1].append(chunk[NCOL : 2 * NCOL])
    field = jnp.concatenate(
        [jnp.concatenate(half, axis=0) for half in halves], axis=1
    ).astype(BF)
    row = iota((256, 256), 0)
    pick = iota((256, 256), 1) == (row & 15) * 16 + (row >> 4)
    out = dot(jnp.where(pick, 1.0, 0.0).astype(BF), field, NT)
    out_ref[...] = out.astype(BF).reshape(16, 16, 384)


def sum_kernel(r_ref, after_ref, out_ref):
    total = r_ref[0].astype(F32)
    for s in range(1, 16):
        total = total + r_ref[s].astype(F32)
    out_ref[...] = total.astype(BF)


def ring_kernel(own_ref, next_ref, prev_ref, far_ref, out_ref):
    even = own_ref[...].astype(F32) + far_ref[...].astype(F32)
    odd = next_ref[...].astype(F32) + prev_ref[...].astype(F32)
    out_ref[...] = (even + odd).astype(BF)


def order_kernel(core_ref, own_ref, xl_ref, core_own_ref, core_xl_ref, out_ref):
    first = core_ref[0] == 0
    mine = own_ref[...].astype(F32) + xl_ref[...].astype(F32)
    other = core_own_ref[...].astype(F32) + core_xl_ref[...].astype(F32)
    low = jnp.where(first, mine, other)
    high = jnp.where(first, other, mine)
    for t in range(9):
        for ih in range(2):
            rows = slice((t * 2 + ih) * 8, (t * 2 + ih) * 8 + 8)
            out_ref[t, 0:8, ih * 128 : ih * 128 + 128] = low[rows]
            out_ref[t, 8:16, ih * 128 : ih * 128 + 128] = high[rows]


def shards(inputs, cotangent, kernel, channel_bias):
    core, z, xh = (
        lax.axis_index(n).astype(jnp.int32).reshape(1) for n in ("core", "z", "xh")
    )
    (packed,) = call(
        pack_kernel,
        [((16, 152, 128), BF)],
        core,
        kernel.reshape(16, 9, 256).transpose(1, 0, 2),
        channel_bias.reshape(1, 16),
        inputs,
        cotangent,
        hbm=(1, 2, 3, 4),
        copied=(0,),
        mib=56,
        scratch=[
            pltpu.VMEM((9, 16, 256), BF),
            pltpu.VMEM((1, 16), F32),
            pltpu.VMEM((16, 16, 384), BF),
            pltpu.VMEM((16, 16, 384), BF),
            pltpu.VMEM((16, 152, 128), BF),
            pltpu.SemaphoreType.DMA((4,)),
            pltpu.SemaphoreType.DMA((3,)),
        ],
    )
    got = lax.all_to_all(packed, CHAN, 0, 0)
    xo, co, ha, w_part = call(
        unpack_kernel,
        [((768, 256), BF), ((512, 128), BF), ((96, 256), BF), ((16, 40, 128), BF)],
        core,
        got,
    )
    across = [(b, b + 1) for b in range(1, 15, 2)]
    across += [(b + 1, b) for b in range(1, 15, 2)]
    xr = lax.ppermute(xo, "core", [(0, 1), (1, 0)])
    ha = lax.ppermute(ha, BAND, across)
    hb = lax.ppermute(ha, "core", [(0, 1), (1, 0)])
    far = [(i, (i + 2) % 8) for i in range(8)] + [(8 + i, 8 + (i + 6) % 8) for i in range(8)]
    (w,) = call(
        weight_kernel,
        [((1152, 256), BF)],
        z,
        w_part,
        lax.ppermute(w_part, "z", [(i, (i + 1) % 8) for i in range(8)]),
        lax.ppermute(w_part, "z", [(i, (i + 7) % 8) for i in range(8)]),
        lax.ppermute(w_part, ("core", "z"), far),
        scratch=[pltpu.VMEM((4, 16, 40, 128), BF)],
    )
    scale = 1.0 / math.sqrt(256 * 384)

    def grads(*refs):
        grad_kernel(scale, *refs)

    kg, g = call(
        grads,
        [((16, 144, 128), BF), ((PX, 128), BF)],
        core,
        xo,
        xr,
        co,
        ha,
        hb,
        w,
        scratch=[
            pltpu.VMEM((1216, 256), BF),
            pltpu.VMEM((1088, 128), BF),
            pltpu.VMEM((PX, 384), F32),
            pltpu.VMEM((PX + 16, 128), F32),
            pltpu.VMEM((16, 144, 128), BF),
            pltpu.SemaphoreType.DMA((3,)),
        ],
        copied=(0,),
    )
    kg = lax.all_to_all(kg, CHAN, 0, 0)
    own, send = call(
        input_kernel,
        [((512, 256), F32), ((512, 256), BF)],
        core,
        g,
        w,
        scratch=[pltpu.VMEM((3, 1056, 256), F32), pltpu.VMEM((1024, 256), F32)],
    )
    recv = lax.ppermute(send, "core", [(0, 1), (1, 0)])
    block = ((8, 48, 128), BF)
    keep, send = call(
        repack_kernel,
        [block, block],
        xh,
        own,
        recv,
        scratch=[pltpu.VMEM((8, 2, 48, 128), BF)],
    )
    recv = lax.ppermute(send, "xh", [(0, 1), (1, 0)])
    (joined,) = call(join_kernel, [((8, 96, 128), BF)], xh, keep, recv)
    back = lax.all_to_all(joined, "z", 0, 0)
    (input_grad,) = call(restore_kernel, [((16, 16, 384), BF)], back, smem=0)

    part = ((144, 128), BF)
    (sums,) = call(sum_kernel, [part], kg, joined, smem=0, hbm=(1,))
    ring = [lax.ppermute(sums, "y", [(i, (i + k) % 4) for i in range(4)]) for k in (3, 1, 2)]
    (sums,) = call(ring_kernel, [part], sums, *ring, smem=0)
    (ordered,) = call(
        order_kernel,
        [((9, 16, 256), F32)],
        core,
        sums,
        lax.ppermute(sums, "xl", [(0, 1), (1, 0)]),
        lax.ppermute(sums, "core", [(0, 1), (1, 0)]),
        lax.ppermute(sums, ("xl", "core"), [(i, i ^ 3) for i in range(4)]),
    )
    kernel_grad = ordered.transpose(1, 0, 2).reshape(16, 3, 3, 256)
    return (input_grad, kernel_grad)


def solution(mesh):
    fine = Mesh(mesh.devices.reshape(2, 4, 2, 8, 2), ("xl", "y", "core", "z", "xh"))
    return jax.shard_map(
        shards,
        mesh=fine,
        in_specs=(
            P(CHAN, BAND, None),
            P(CHAN, BAND, None),
            P(CHAN, None, None, None),
            P(CHAN),
        ),
        out_specs=(P(CHAN, BAND, None), P(CHAN, None, None, None)),
        check_vma=False,
    )
```

```python
import math

import jax
import jax.numpy as jnp
from jax import lax
from jax.experimental import pallas as pl
from jax.experimental.pallas import tpu as pltpu
from jax.sharding import Mesh
from jax.sharding import PartitionSpec as P

BF = jnp.bfloat16
F32 = jnp.float32
CHAN = ("z", "xh")
BAND = ("xl", "y", "core")
PITCH = 32
NCOL = 24
PX = 1152
NT = (((1,), (1,)), ((), ()))
TN = (((0,), (0,)), ((), ()))


def dot(a, b, dims=(((1,), (0,)), ((), ()))):
    return lax.dot_general(a, b, dims, preferred_element_type=F32)


def iota(shape, dim):
    return lax.broadcasted_iota(jnp.int32, shape, dim)


def call(body, outs, *args, smem=1, scratch=(), hbm=(), copied=(), mib=48):
    specs = [
        pl.BlockSpec(
            memory_space=pltpu.SMEM if k < smem else pltpu.HBM if k in hbm else pltpu.VMEM
        )
        for k in range(len(args))
    ]
    return pl.pallas_call(
        body,
        out_shape=[jax.ShapeDtypeStruct(s, d) for s, d in outs],
        in_specs=specs,
        out_specs=[
            pl.BlockSpec(memory_space=pltpu.HBM if k in copied else pltpu.VMEM)
            for k in range(len(outs))
        ],
        scratch_shapes=list(scratch),
        compiler_params=pltpu.CompilerParams(vmem_limit_bytes=mib * 1024 * 1024),
    )(*args)


def swap_blocks(arrays, block):
    lanes = arrays[0].shape[1]
    place = iota(arrays[0].shape, 1) // block
    bit = 1
    while bit < len(arrays):
        upper = (place & bit) != 0
        out = list(arrays)
        for s in range(len(arrays)):
            if s & bit:
                continue
            a, b = arrays[s], arrays[s | bit]
            out[s] = jnp.where(upper, pltpu.roll(b, bit * block, 1), a)
            out[s | bit] = jnp.where(upper, b, pltpu.roll(a, lanes - bit * block, 1))
        arrays = out
        bit *= 2
    return arrays


def window(first, count):
    row = iota((512, 1), 0)
    c = row & 31
    column = jnp.where(c < count, (row >> 5) * NCOL + c + first, -1)
    return jnp.where(iota((512, 384), 1) == column, 1.0, 0.0).astype(BF)


def half_up(tile):
    return pltpu.roll(tile, 4, tile.ndim - 2)


def fold(field):
    low = iota((16, 8, 128), 1) < 4
    rest = jnp.where(low, field[:, 24:32, 0:128], half_up(field[:, 24:32, 128:256]))
    return [field[:, 0:24, 0:128], field[:, 0:24, 128:256], rest]


def unfold(chunk):
    rest = chunk[48:56]
    return [
        jnp.concatenate([chunk[0:24], rest], axis=0).astype(BF),
        jnp.concatenate([chunk[24:48], half_up(rest)], axis=0).astype(BF),
    ]


def copy_rows(buffer, out, first, last, sem):
    rows = pl.ds(first, last - first)
    copy = pltpu.make_async_copy(buffer.at[:, rows, :], out.at[:, rows, :], sem)
    copy.start()
    return copy


def pack_kernel(core_ref, *refs):
    out_hbm, buffer, sems, out_sems = refs[4], refs[9], refs[10], refs[11]
    copies = [pltpu.make_async_copy(refs[k], refs[5 + k], sems.at[k]) for k in range(4)]
    for copy in copies:
        copy.start()
    ker_ref, bias_ref, x_ref, cot_ref = refs[5:9]
    core = core_ref[0]
    dst = iota((256, 256), 0)
    src = iota((256, 256), 1)
    ch, h = src >> 4, src & 15
    to_h_ch = jnp.where(dst == h * 16 + ch, 1.0, 0.0).astype(BF)
    other = (ch >> 3) ^ core
    to_half = jnp.where(dst == other * 128 + h * 8 + (ch & 7), 1.0, 0.0).astype(BF)
    x_window = window(-2, 28)
    cot_window = window(-1, 26)

    copies[0].wait()
    upper = iota((8, 256), 0) < 4
    mine = []
    for t in range(9):
        both = ker_ref[t].astype(F32)
        mine.append(jnp.where(core == 0, both[0:8], both[8:16]))
    halves = []
    for r in range(2):
        taps = [mine[t] if (t % 2 == r) else half_up(mine[t]) for t in range(9)] + [mine[8]]
        pairs = [jnp.where(upper, taps[t], taps[t + 1]) for t in range(0, 10, 2)]
        halves.append(jnp.concatenate(pairs, axis=0))
    copies[1].wait()
    bias = jnp.broadcast_to(bias_ref[...], (8, 16))
    hi = bias.astype(BF).astype(F32)
    mid = (bias - hi).astype(BF).astype(F32)
    low = bias - hi - mid
    k = iota((8, 16), 0)
    pieces = jnp.where(k == 2, hi, jnp.where(k == 3, mid, jnp.where(k == 6, low, 0.0)))
    spread = iota((16, 128), 0) == (core * 8 + (iota((16, 128), 1) & 7))
    pieces = dot(pieces.astype(BF), jnp.where(spread, 1.0, 0.0).astype(BF))

    copies[2].wait()
    copies[3].wait()
    x = dot(to_h_ch, x_ref[...].reshape(256, 384)).astype(BF)
    x = fold(dot(x_window, x, NT).reshape(16, 32, 256))
    c = dot(to_half, cot_ref[...].reshape(256, 384)).astype(BF)
    c = fold(dot(cot_window, c, NT).reshape(16, 32, 256))
    c[2] = c[2] + pieces[None]
    field = jnp.concatenate(x + c, axis=1)
    sent = []
    for first in range(0, 16, 4):
        for j in range(first, first + 4):
            lane = (j // 2 % 2) * 128
            quarter = halves[j // 4 % 2][:, lane : lane + 128]
            buffer[j] = jnp.concatenate([field[j], quarter], axis=0).astype(BF)
        slabs = pl.ds(first, 4)
        copy = pltpu.make_async_copy(buffer.at[slabs], out_hbm.at[slabs], out_sems.at[first // 4])
        copy.start()
        sent.append(copy)
    for copy in sent:
        copy.wait()


SOURCES = [z * 2 + xh for xh in range(2) for z in range(8)]


def unpack_kernel(core_ref, r_ref, xo_ref, co_ref, ha_ref, w_ref):
    core = core_ref[0]
    edge = []
    chunks = [r_ref[s].astype(F32) for s in range(16)]
    fields = [unfold(chunk[0:56]) for chunk in chunks]
    for hh in range(2):
        halves = []
        for sh in range(2):
            halves.append(swap_blocks([fields[sh * 8 + s][hh] for s in range(8)], 16))
        for hl in range(8):
            at = (hh * 8 + hl) * 32
            row = jnp.concatenate([halves[0][hl], halves[1][hl]], axis=1)
            xo_ref[at : at + 32, :] = row
            if (hh * 8 + hl) in (0, 1, 14, 15):
                edge.append(row)
    cots = [unfold(chunks[s][56:112]) for s in SOURCES]
    own = swap_blocks([cot[0] for cot in cots], 8)
    oth = swap_blocks([cot[1] for cot in cots], 8)
    for h in range(16):
        co_ref[h * 32 : h * 32 + 32, :] = own[h]
        at = 512 + (h % 8) * 32
        xo_ref[at : at + 32, (h // 8) * 128 : (h // 8) * 128 + 128] = oth[h]
    first = core == 0
    ha_ref[0:32, :] = jnp.where(first, edge[0], edge[2])
    ha_ref[32:64, :] = jnp.where(first, edge[1], edge[3])
    ha_ref[64:96, 0:128] = jnp.where(first, oth[0], oth[15])
    ha_ref[64:96, 128:256] = jnp.where(first, own[0], own[15])
    for k in range(16):
        w_ref[k] = chunks[SOURCES[k]][112:152].astype(BF)


def weight_kernel(z_ref, own_ref, below_ref, above_ref, far_ref, w_ref, quarters):
    for ref, offset in ((own_ref, 0), (below_ref, 3), (above_ref, 1), (far_ref, 2)):
        quarters[(z_ref[0] + offset) & 3] = ref[...]
    upper = iota((16, 8, 128), 1) < 4
    for ih in range(2):
        first, second = quarters[ih].astype(F32), quarters[2 + ih].astype(F32)
        for t in range(9):
            rows = slice((t // 2) * 8, (t // 2) * 8 + 8)
            if t % 2 == 0:
                tap = jnp.where(upper, first[:, rows], half_up(second[:, rows]))
            else:
                tap = jnp.where(upper, half_up(first[:, rows]), second[:, rows])
            w_ref[t * 128 : t * 128 + 128, ih * 128 : ih * 128 + 128] = tap.reshape(
                128, 128
            ).astype(BF)


def grad_kernel(scale, core_ref, xo_ref, xr_ref, co_ref, ha_ref, hb_ref, w_ref, *refs):
    kg_hbm, g_ref, x, cot, y, gs, buffer, sems = refs
    core = core_ref[0]
    first = core == 0
    mine = pl.multiple_of(core * 512, 512)
    theirs = pl.multiple_of((1 - core) * 512, 512)
    x[0:64, :] = jnp.where(first, ha_ref[0:64, :], hb_ref[0:64, :])
    x[pl.ds(64 + mine, 512), :] = xo_ref[0:512, :]
    x[pl.ds(64 + theirs, 512), :] = xr_ref[0:512, :]
    x[1088:1152, :] = jnp.where(first, hb_ref[0:64, :], ha_ref[0:64, :])
    x[1152:1216, :] = jnp.zeros((64, 256), BF)
    cot[0:32, :] = jnp.where(first, ha_ref[64:96, 0:128], hb_ref[64:96, 128:256])
    cot[pl.ds(32 + mine, 512), :] = co_ref[...]
    cot[pl.ds(32 + theirs, 256), :] = xr_ref[512:768, 0:128]
    cot[pl.ds(32 + theirs + 256, 256), :] = xr_ref[512:768, 128:256]
    cot[1056:1088, :] = jnp.where(first, hb_ref[64:96, 128:256], ha_ref[64:96, 0:128])

    bias = co_ref[16:32, :].astype(F32)
    bias = bias[10:11] + bias[11:12] + bias[14:15]

    for m in range(0, PX, 384):
        y[m : m + 384, :] = (
            dot(x[m : m + 384, :], w_ref[0:384, :], NT)
            + dot(x[m + 32 : m + 416, :], w_ref[384:768, :], NT)
            + dot(x[m + 64 : m + 448, :], w_ref[768:1152, :], NT)
        )

    gs[0:16, :] = jnp.zeros((16, 128), F32)
    for m in range(0, 1088, 64):
        pre = (
            y[m : m + 64, 0:128]
            + y[m + 1 : m + 65, 128:256]
            + y[m + 2 : m + 66, 256:384]
            + bias
        )
        s = 1.0 / (1.0 + jnp.exp(-pre))
        c = iota((64, 128), 0) & 31
        grad = cot[m : m + 64, :].astype(F32) * s * (1.0 + pre * (1.0 - s))
        grad = jnp.where(c < 26, grad, 0.0).astype(BF)
        g_ref[m : m + 64, :] = grad
        p = iota((64, 128), 0) + m
        inner = (c >= 1) & (c <= NCOL) & (p >= 32) & (p < 1056)
        gs[16 + m : 16 + m + 64, :] = jnp.where(inner, grad.astype(F32), 0.0)
    g_ref[1088:PX, :] = jnp.zeros((PX - 1088, 128), BF)
    gs[16 + 1088 : 16 + PX, :] = jnp.zeros((PX - 1088, 128), F32)

    shifted = jnp.concatenate(
        [gs[16 - b : 16 - b + PX, :].astype(BF) for b in range(3)], axis=1
    )
    sent = []
    for a in range(3):
        block = dot(shifted, x[32 * a : 32 * a + PX, :], TN) * scale
        for k in range(16):
            rows = []
            for b in range(3):
                tap = block[128 * b + 8 * k : 128 * b + 8 * k + 8]
                rows += [tap[:, 0:128], tap[:, 128:256]]
            buffer[SOURCES[k], 48 * a : 48 * a + 48, :] = jnp.concatenate(rows, axis=0).astype(BF)
        sent.append(copy_rows(buffer, kg_hbm, 48 * a, 48 * a + 48, sems.at[a]))
    for copy in sent:
        copy.wait()


def input_kernel(core_ref, g_ref, w_ref, own_ref, send_ref, z, total):
    core = core_ref[0]
    for m in (0, 352, 704):
        for b in range(3):
            z[b, m : m + 352, :] = (
                dot(g_ref[m + 64 : m + 416, :], w_ref[b * 128 : b * 128 + 128, :])
                + dot(g_ref[m + 32 : m + 384, :], w_ref[384 + b * 128 : 512 + b * 128, :])
                + dot(g_ref[m : m + 352, :], w_ref[768 + b * 128 : 896 + b * 128, :])
            )
    for m in range(0, 1024, 64):
        total[m : m + 64, :] = (
            z[0, m + 2 : m + 66, :] + z[1, m + 1 : m + 65, :] + z[2, m : m + 64, :]
        )
    own_ref[...] = total[pl.ds(pl.multiple_of(core * 512, 512), 512), :]
    send_ref[...] = total[pl.ds(pl.multiple_of((1 - core) * 512, 512), 512), :].astype(BF)


def repack_kernel(xh_ref, own_ref, recv_ref, keep_ref, send_ref, chunks):
    parts = []
    for hh in range(2):
        rows = []
        for hl in range(8):
            at = (hh * 8 + hl) * 32
            row = own_ref[at : at + 32, :] + recv_ref[at : at + 32, :].astype(F32)
            rows.append(row[0:NCOL])
        parts.append([swap_blocks([r[:, q : q + 128] for r in rows], 16) for q in (0, 128)])
    for d in range(16):
        chunks[d // 2, d % 2] = jnp.concatenate(
            [parts[0][d // 8][d % 8], parts[1][d // 8][d % 8]], axis=0
        ).astype(BF)
    keep_ref[...] = chunks[:, pl.ds(xh_ref[0], 1)].reshape(8, 48, 128)
    send_ref[...] = chunks[:, pl.ds(1 - xh_ref[0], 1)].reshape(8, 48, 128)


def join_kernel(xh_ref, keep_ref, recv_ref, out_ref):
    first = xh_ref[0] == 0
    out_ref[:, 0:48, :] = jnp.where(first, keep_ref[...], recv_ref[...])
    out_ref[:, 48:96, :] = jnp.where(first, recv_ref[...], keep_ref[...])


def restore_kernel(r_ref, out_ref):
    halves = [[], []]
    for j in range(16):
        chunk = r_ref[j // 2, (j % 2) * 48 : (j % 2) * 48 + 48, :].astype(F32)
        halves[0].append(chunk[0:NCOL])
        halves[1].append(chunk[NCOL : 2 * NCOL])
    field = jnp.concatenate(
        [jnp.concatenate(half, axis=0) for half in halves], axis=1
    ).astype(BF)
    row = iota((256, 256), 0)
    pick = iota((256, 256), 1) == (row & 15) * 16 + (row >> 4)
    out = dot(jnp.where(pick, 1.0, 0.0).astype(BF), field, NT)
    out_ref[...] = out.astype(BF).reshape(16, 16, 384)


def sum_kernel(r_ref, after_ref, out_ref):
    total = r_ref[0].astype(F32)
    for s in range(1, 16):
        total = total + r_ref[s].astype(F32)
    out_ref[...] = total.astype(BF)


def ring_kernel(own_ref, next_ref, prev_ref, far_ref, out_ref):
    even = own_ref[...].astype(F32) + far_ref[...].astype(F32)
    odd = next_ref[...].astype(F32) + prev_ref[...].astype(F32)
    out_ref[...] = (even + odd).astype(BF)


def order_kernel(core_ref, own_ref, xl_ref, core_own_ref, core_xl_ref, out_ref):
    first = core_ref[0] == 0
    mine = own_ref[...].astype(F32) + xl_ref[...].astype(F32)
    other = core_own_ref[...].astype(F32) + core_xl_ref[...].astype(F32)
    low = jnp.where(first, mine, other)
    high = jnp.where(first, other, mine)
    for t in range(9):
        for ih in range(2):
            rows = slice((t * 2 + ih) * 8, (t * 2 + ih) * 8 + 8)
            out_ref[t, 0:8, ih * 128 : ih * 128 + 128] = low[rows]
            out_ref[t, 8:16, ih * 128 : ih * 128 + 128] = high[rows]


def shards(inputs, cotangent, kernel, channel_bias):
    core, z, xh = (
        lax.axis_index(n).astype(jnp.int32).reshape(1) for n in ("core", "z", "xh")
    )
    (packed,) = call(
        pack_kernel,
        [((16, 152, 128), BF)],
        core,
        kernel.reshape(16, 9, 256).transpose(1, 0, 2),
        channel_bias.reshape(1, 16),
        inputs,
        cotangent,
        hbm=(1, 2, 3, 4),
        copied=(0,),
        mib=56,
        scratch=[
            pltpu.VMEM((9, 16, 256), BF),
            pltpu.VMEM((1, 16), F32),
            pltpu.VMEM((16, 16, 384), BF),
            pltpu.VMEM((16, 16, 384), BF),
            pltpu.VMEM((16, 152, 128), BF),
            pltpu.SemaphoreType.DMA((4,)),
            pltpu.SemaphoreType.DMA((4,)),
        ],
    )
    got = lax.all_to_all(packed, CHAN, 0, 0)
    xo, co, ha, w_part = call(
        unpack_kernel,
        [((768, 256), BF), ((512, 128), BF), ((96, 256), BF), ((16, 40, 128), BF)],
        core,
        got,
    )
    across = [(b, b + 1) for b in range(1, 15, 2)]
    across += [(b + 1, b) for b in range(1, 15, 2)]
    xr = lax.ppermute(xo, "core", [(0, 1), (1, 0)])
    ha = lax.ppermute(ha, BAND, across)
    hb = lax.ppermute(ha, "core", [(0, 1), (1, 0)])
    far = [(i, (i + 2) % 8) for i in range(8)] + [(8 + i, 8 + (i + 6) % 8) for i in range(8)]
    (w,) = call(
        weight_kernel,
        [((1152, 256), BF)],
        z,
        w_part,
        lax.ppermute(w_part, "z", [(i, (i + 1) % 8) for i in range(8)]),
        lax.ppermute(w_part, "z", [(i, (i + 7) % 8) for i in range(8)]),
        lax.ppermute(w_part, ("core", "z"), far),
        scratch=[pltpu.VMEM((4, 16, 40, 128), BF)],
    )
    scale = 1.0 / math.sqrt(256 * 384)

    def grads(*refs):
        grad_kernel(scale, *refs)

    kg, g = call(
        grads,
        [((16, 144, 128), BF), ((PX, 128), BF)],
        core,
        xo,
        xr,
        co,
        ha,
        hb,
        w,
        scratch=[
            pltpu.VMEM((1216, 256), BF),
            pltpu.VMEM((1088, 128), BF),
            pltpu.VMEM((PX, 384), F32),
            pltpu.VMEM((PX + 16, 128), F32),
            pltpu.VMEM((16, 144, 128), BF),
            pltpu.SemaphoreType.DMA((3,)),
        ],
        copied=(0,),
    )
    kg = lax.all_to_all(kg, CHAN, 0, 0)
    own, send = call(
        input_kernel,
        [((512, 256), F32), ((512, 256), BF)],
        core,
        g,
        w,
        scratch=[pltpu.VMEM((3, 1056, 256), F32), pltpu.VMEM((1024, 256), F32)],
    )
    recv = lax.ppermute(send, "core", [(0, 1), (1, 0)])
    block = ((8, 48, 128), BF)
    keep, send = call(
        repack_kernel,
        [block, block],
        xh,
        own,
        recv,
        scratch=[pltpu.VMEM((8, 2, 48, 128), BF)],
    )
    recv = lax.ppermute(send, "xh", [(0, 1), (1, 0)])
    (joined,) = call(join_kernel, [((8, 96, 128), BF)], xh, keep, recv)
    back = lax.all_to_all(joined, "z", 0, 0)
    (input_grad,) = call(restore_kernel, [((16, 16, 384), BF)], back, smem=0)

    part = ((144, 128), BF)
    (sums,) = call(sum_kernel, [part], kg, joined, smem=0, hbm=(1,))
    ring = [lax.ppermute(sums, "y", [(i, (i + k) % 4) for i in range(4)]) for k in (3, 1, 2)]
    (sums,) = call(ring_kernel, [part], sums, *ring, smem=0)
    (ordered,) = call(
        order_kernel,
        [((9, 16, 256), F32)],
        core,
        sums,
        lax.ppermute(sums, "xl", [(0, 1), (1, 0)]),
        lax.ppermute(sums, "core", [(0, 1), (1, 0)]),
        lax.ppermute(sums, ("xl", "core"), [(i, i ^ 3) for i in range(4)]),
    )
    kernel_grad = ordered.transpose(1, 0, 2).reshape(16, 3, 3, 256)
    return (input_grad, kernel_grad)


def solution(mesh):
    fine = Mesh(mesh.devices.reshape(2, 4, 2, 8, 2), ("xl", "y", "core", "z", "xh"))
    return jax.shard_map(
        shards,
        mesh=fine,
        in_specs=(
            P(CHAN, BAND, None),
            P(CHAN, BAND, None),
            P(CHAN, None, None, None),
            P(CHAN),
        ),
        out_specs=(P(CHAN, BAND, None), P(CHAN, None, None, None)),
        check_vma=False,
    )
```

```python
import math

import jax
import jax.numpy as jnp
from jax import lax
from jax.experimental import pallas as pl
from jax.experimental.pallas import tpu as pltpu
from jax.sharding import Mesh
from jax.sharding import PartitionSpec as P

BF = jnp.bfloat16
F32 = jnp.float32
CHAN = ("z", "xh")
SLOTS = ("xh", "z")
BAND = ("xl", "y", "core")
PITCH = 32
NCOL = 24
PX = 1152
NT = (((1,), (1,)), ((), ()))
TN = (((0,), (0,)), ((), ()))


def dot(a, b, dims=(((1,), (0,)), ((), ()))):
    return lax.dot_general(a, b, dims, preferred_element_type=F32)


def iota(shape, dim):
    return lax.broadcasted_iota(jnp.int32, shape, dim)


def call(body, outs, *args, smem=1, scratch=(), hbm=(), copied=(), mib=48):
    specs = [
        pl.BlockSpec(
            memory_space=pltpu.SMEM if k < smem else pltpu.HBM if k in hbm else pltpu.VMEM
        )
        for k in range(len(args))
    ]
    return pl.pallas_call(
        body,
        out_shape=[jax.ShapeDtypeStruct(s, d) for s, d in outs],
        in_specs=specs,
        out_specs=[
            pl.BlockSpec(memory_space=pltpu.HBM if k in copied else pltpu.VMEM)
            for k in range(len(outs))
        ],
        scratch_shapes=list(scratch),
        compiler_params=pltpu.CompilerParams(vmem_limit_bytes=mib * 1024 * 1024),
    )(*args)


def swap_blocks(arrays, block):
    lanes = arrays[0].shape[1]
    place = iota(arrays[0].shape, 1) // block
    bit = 1
    while bit < len(arrays):
        upper = (place & bit) != 0
        out = list(arrays)
        for s in range(len(arrays)):
            if s & bit:
                continue
            a, b = arrays[s], arrays[s | bit]
            out[s] = jnp.where(upper, pltpu.roll(b, bit * block, 1), a)
            out[s | bit] = jnp.where(upper, b, pltpu.roll(a, lanes - bit * block, 1))
        arrays = out
        bit *= 2
    return arrays


def window(first, count):
    row = iota((512, 1), 0)
    c = row & 31
    column = jnp.where(c < count, (row >> 5) * NCOL + c + first, -1)
    return jnp.where(iota((512, 384), 1) == column, 1.0, 0.0).astype(BF)


def half_up(tile):
    return pltpu.roll(tile, 4, tile.ndim - 2)


def fold(field):
    low = iota((16, 8, 128), 1) < 4
    rest = jnp.where(low, field[:, 24:32, 0:128], half_up(field[:, 24:32, 128:256]))
    return [field[:, 0:24, 0:128], field[:, 0:24, 128:256], rest]


def unfold(chunk):
    rest = chunk[48:56]
    return [
        jnp.concatenate([chunk[0:24], rest], axis=0).astype(BF),
        jnp.concatenate([chunk[24:48], half_up(rest)], axis=0).astype(BF),
    ]


def copy_rows(buffer, out, first, last, sem):
    rows = pl.ds(first, last - first)
    copy = pltpu.make_async_copy(buffer.at[:, rows, :], out.at[:, rows, :], sem)
    copy.start()
    return copy


def pack_kernel(core_ref, *refs):
    out_hbm, buffer, sems, out_sems = refs[4], refs[9], refs[10], refs[11]
    copies = [pltpu.make_async_copy(refs[k], refs[5 + k], sems.at[k]) for k in range(4)]
    for copy in copies:
        copy.start()
    ker_ref, bias_ref, x_ref, cot_ref = refs[5:9]
    core = core_ref[0]
    dst = iota((256, 256), 0)
    src = iota((256, 256), 1)
    ch, h = src >> 4, src & 15
    to_h_ch = jnp.where(dst == h * 16 + ch, 1.0, 0.0).astype(BF)
    other = (ch >> 3) ^ core
    to_half = jnp.where(dst == other * 128 + h * 8 + (ch & 7), 1.0, 0.0).astype(BF)
    x_window = window(-2, 28)
    cot_window = window(-1, 26)

    copies[0].wait()
    upper = iota((8, 256), 0) < 4
    mine = []
    for t in range(9):
        both = ker_ref[t].astype(F32)
        mine.append(jnp.where(core == 0, both[0:8], both[8:16]))
    halves = []
    for r in range(2):
        taps = [mine[t] if (t % 2 == r) else half_up(mine[t]) for t in range(9)] + [mine[8]]
        pairs = [jnp.where(upper, taps[t], taps[t + 1]) for t in range(0, 10, 2)]
        halves.append(jnp.concatenate(pairs, axis=0))
    copies[1].wait()
    bias = jnp.broadcast_to(bias_ref[...], (8, 16))
    hi = bias.astype(BF).astype(F32)
    mid = (bias - hi).astype(BF).astype(F32)
    low = bias - hi - mid
    k = iota((8, 16), 0)
    pieces = jnp.where(k == 2, hi, jnp.where(k == 3, mid, jnp.where(k == 6, low, 0.0)))
    spread = iota((16, 128), 0) == (core * 8 + (iota((16, 128), 1) & 7))
    pieces = dot(pieces.astype(BF), jnp.where(spread, 1.0, 0.0).astype(BF))

    copies[2].wait()
    copies[3].wait()
    x = dot(to_h_ch, x_ref[...].reshape(256, 384)).astype(BF)
    x = fold(dot(x_window, x, NT).reshape(16, 32, 256))
    c = dot(to_half, cot_ref[...].reshape(256, 384)).astype(BF)
    c = fold(dot(cot_window, c, NT).reshape(16, 32, 256))
    c[2] = c[2] + pieces[None]
    field = jnp.concatenate(x + c, axis=1)
    sent = []
    for first in range(0, 16, 4):
        for k in range(first, first + 4):
            j = SOURCES[k]
            lane = (j // 2 % 2) * 128
            quarter = halves[j // 4 % 2][:, lane : lane + 128]
            buffer[k] = jnp.concatenate([field[j], quarter], axis=0).astype(BF)
        slabs = pl.ds(first, 4)
        copy = pltpu.make_async_copy(buffer.at[slabs], out_hbm.at[slabs], out_sems.at[first // 4])
        copy.start()
        sent.append(copy)
    for copy in sent:
        copy.wait()


SOURCES = [z * 2 + xh for xh in range(2) for z in range(8)]


def unpack_kernel(core_ref, r_ref, xo_ref, co_ref, ha_ref, w_ref):
    core = core_ref[0]
    edge = []
    chunks = [r_ref[s % 2 * 8 + s // 2].astype(F32) for s in range(16)]
    fields = [unfold(chunk[0:56]) for chunk in chunks]
    for hh in range(2):
        halves = []
        for sh in range(2):
            halves.append(swap_blocks([fields[sh * 8 + s][hh] for s in range(8)], 16))
        for hl in range(8):
            at = (hh * 8 + hl) * 32
            row = jnp.concatenate([halves[0][hl], halves[1][hl]], axis=1)
            xo_ref[at : at + 32, :] = row
            if (hh * 8 + hl) in (0, 1, 14, 15):
                edge.append(row)
    cots = [unfold(chunks[s][56:112]) for s in SOURCES]
    own = swap_blocks([cot[0] for cot in cots], 8)
    oth = swap_blocks([cot[1] for cot in cots], 8)
    for h in range(16):
        co_ref[h * 32 : h * 32 + 32, :] = own[h]
        at = 512 + (h % 8) * 32
        xo_ref[at : at + 32, (h // 8) * 128 : (h // 8) * 128 + 128] = oth[h]
    first = core == 0
    ha_ref[0:32, :] = jnp.where(first, edge[0], edge[2])
    ha_ref[32:64, :] = jnp.where(first, edge[1], edge[3])
    ha_ref[64:96, 0:128] = jnp.where(first, oth[0], oth[15])
    ha_ref[64:96, 128:256] = jnp.where(first, own[0], own[15])
    for k in range(16):
        w_ref[k] = chunks[SOURCES[k]][112:152].astype(BF)


def weight_kernel(z_ref, own_ref, below_ref, above_ref, far_ref, w_ref, quarters):
    for ref, offset in ((own_ref, 0), (below_ref, 3), (above_ref, 1), (far_ref, 2)):
        quarters[(z_ref[0] + offset) & 3] = ref[...]
    upper = iota((16, 8, 128), 1) < 4
    for ih in range(2):
        first, second = quarters[ih].astype(F32), quarters[2 + ih].astype(F32)
        for t in range(9):
            rows = slice((t // 2) * 8, (t // 2) * 8 + 8)
            if t % 2 == 0:
                tap = jnp.where(upper, first[:, rows], half_up(second[:, rows]))
            else:
                tap = jnp.where(upper, half_up(first[:, rows]), second[:, rows])
            w_ref[t * 128 : t * 128 + 128, ih * 128 : ih * 128 + 128] = tap.reshape(
                128, 128
            ).astype(BF)


def grad_kernel(scale, core_ref, xo_ref, xr_ref, co_ref, ha_ref, hb_ref, w_ref, *refs):
    kg_hbm, g_ref, x, cot, y, gs, buffer, sems = refs
    core = core_ref[0]
    first = core == 0
    mine = pl.multiple_of(core * 512, 512)
    theirs = pl.multiple_of((1 - core) * 512, 512)
    x[0:64, :] = jnp.where(first, ha_ref[0:64, :], hb_ref[0:64, :])
    x[pl.ds(64 + mine, 512), :] = xo_ref[0:512, :]
    x[pl.ds(64 + theirs, 512), :] = xr_ref[0:512, :]
    x[1088:1152, :] = jnp.where(first, hb_ref[0:64, :], ha_ref[0:64, :])
    x[1152:1216, :] = jnp.zeros((64, 256), BF)
    cot[0:32, :] = jnp.where(first, ha_ref[64:96, 0:128], hb_ref[64:96, 128:256])
    cot[pl.ds(32 + mine, 512), :] = co_ref[...]
    cot[pl.ds(32 + theirs, 256), :] = xr_ref[512:768, 0:128]
    cot[pl.ds(32 + theirs + 256, 256), :] = xr_ref[512:768, 128:256]
    cot[1056:1088, :] = jnp.where(first, hb_ref[64:96, 128:256], ha_ref[64:96, 0:128])

    bias = co_ref[16:32, :].astype(F32)
    bias = bias[10:11] + bias[11:12] + bias[14:15]

    for m in range(0, PX, 384):
        y[m : m + 384, :] = (
            dot(x[m : m + 384, :], w_ref[0:384, :], NT)
            + dot(x[m + 32 : m + 416, :], w_ref[384:768, :], NT)
            + dot(x[m + 64 : m + 448, :], w_ref[768:1152, :], NT)
        )

    gs[0:16, :] = jnp.zeros((16, 128), F32)
    for m in range(0, 1088, 64):
        pre = (
            y[m : m + 64, 0:128]
            + y[m + 1 : m + 65, 128:256]
            + y[m + 2 : m + 66, 256:384]
            + bias
        )
        s = 1.0 / (1.0 + jnp.exp(-pre))
        c = iota((64, 128), 0) & 31
        grad = cot[m : m + 64, :].astype(F32) * s * (1.0 + pre * (1.0 - s))
        grad = jnp.where(c < 26, grad, 0.0).astype(BF)
        g_ref[m : m + 64, :] = grad
        p = iota((64, 128), 0) + m
        inner = (c >= 1) & (c <= NCOL) & (p >= 32) & (p < 1056)
        gs[16 + m : 16 + m + 64, :] = jnp.where(inner, grad.astype(F32), 0.0)
    g_ref[1088:PX, :] = jnp.zeros((PX - 1088, 128), BF)
    gs[16 + 1088 : 16 + PX, :] = jnp.zeros((PX - 1088, 128), F32)

    shifted = jnp.concatenate(
        [gs[16 - b : 16 - b + PX, :].astype(BF) for b in range(3)], axis=1
    )
    sent = []
    for a in range(3):
        block = dot(shifted, x[32 * a : 32 * a + PX, :], TN) * scale
        for k in range(16):
            rows = []
            for b in range(3):
                tap = block[128 * b + 8 * k : 128 * b + 8 * k + 8]
                rows += [tap[:, 0:128], tap[:, 128:256]]
            buffer[k, 48 * a : 48 * a + 48, :] = jnp.concatenate(rows, axis=0).astype(BF)
        sent.append(copy_rows(buffer, kg_hbm, 48 * a, 48 * a + 48, sems.at[a]))
    for copy in sent:
        copy.wait()


def input_kernel(core_ref, g_ref, w_ref, own_ref, send_ref, z, total):
    core = core_ref[0]
    for m in (0, 352, 704):
        for b in range(3):
            z[b, m : m + 352, :] = (
                dot(g_ref[m + 64 : m + 416, :], w_ref[b * 128 : b * 128 + 128, :])
                + dot(g_ref[m + 32 : m + 384, :], w_ref[384 + b * 128 : 512 + b * 128, :])
                + dot(g_ref[m : m + 352, :], w_ref[768 + b * 128 : 896 + b * 128, :])
            )
    for m in range(0, 1024, 64):
        total[m : m + 64, :] = (
            z[0, m + 2 : m + 66, :] + z[1, m + 1 : m + 65, :] + z[2, m : m + 64, :]
        )
    own_ref[...] = total[pl.ds(pl.multiple_of(core * 512, 512), 512), :]
    send_ref[...] = total[pl.ds(pl.multiple_of((1 - core) * 512, 512), 512), :].astype(BF)


def repack_kernel(xh_ref, own_ref, recv_ref, keep_ref, send_ref, chunks):
    parts = []
    for hh in range(2):
        rows = []
        for hl in range(8):
            at = (hh * 8 + hl) * 32
            row = own_ref[at : at + 32, :] + recv_ref[at : at + 32, :].astype(F32)
            rows.append(row[0:NCOL])
        parts.append([swap_blocks([r[:, q : q + 128] for r in rows], 16) for q in (0, 128)])
    for d in range(16):
        chunks[d // 2, d % 2] = jnp.concatenate(
            [parts[0][d // 8][d % 8], parts[1][d // 8][d % 8]], axis=0
        ).astype(BF)
    keep_ref[...] = chunks[:, pl.ds(xh_ref[0], 1)].reshape(8, 48, 128)
    send_ref[...] = chunks[:, pl.ds(1 - xh_ref[0], 1)].reshape(8, 48, 128)


def join_kernel(xh_ref, keep_ref, recv_ref, out_ref):
    first = xh_ref[0] == 0
    out_ref[:, 0:48, :] = jnp.where(first, keep_ref[...], recv_ref[...])
    out_ref[:, 48:96, :] = jnp.where(first, recv_ref[...], keep_ref[...])


def restore_kernel(r_ref, out_ref):
    halves = [[], []]
    for j in range(16):
        chunk = r_ref[j // 2, (j % 2) * 48 : (j % 2) * 48 + 48, :].astype(F32)
        halves[0].append(chunk[0:NCOL])
        halves[1].append(chunk[NCOL : 2 * NCOL])
    field = jnp.concatenate(
        [jnp.concatenate(half, axis=0) for half in halves], axis=1
    ).astype(BF)
    row = iota((256, 256), 0)
    pick = iota((256, 256), 1) == (row & 15) * 16 + (row >> 4)
    out = dot(jnp.where(pick, 1.0, 0.0).astype(BF), field, NT)
    out_ref[...] = out.astype(BF).reshape(16, 16, 384)


def sum_kernel(r_ref, after_ref, out_ref):
    total = r_ref[0].astype(F32)
    for s in range(1, 16):
        total = total + r_ref[s].astype(F32)
    out_ref[...] = total.astype(BF)


def ring_kernel(own_ref, next_ref, prev_ref, far_ref, out_ref):
    even = own_ref[...].astype(F32) + far_ref[...].astype(F32)
    odd = next_ref[...].astype(F32) + prev_ref[...].astype(F32)
    out_ref[...] = (even + odd).astype(BF)


def order_kernel(core_ref, own_ref, xl_ref, core_own_ref, core_xl_ref, out_ref):
    first = core_ref[0] == 0
    mine = own_ref[...].astype(F32) + xl_ref[...].astype(F32)
    other = core_own_ref[...].astype(F32) + core_xl_ref[...].astype(F32)
    low = jnp.where(first, mine, other)
    high = jnp.where(first, other, mine)
    for t in range(9):
        for ih in range(2):
            rows = slice((t * 2 + ih) * 8, (t * 2 + ih) * 8 + 8)
            out_ref[t, 0:8, ih * 128 : ih * 128 + 128] = low[rows]
            out_ref[t, 8:16, ih * 128 : ih * 128 + 128] = high[rows]


def shards(inputs, cotangent, kernel, channel_bias):
    core, z, xh = (
        lax.axis_index(n).astype(jnp.int32).reshape(1) for n in ("core", "z", "xh")
    )
    (packed,) = call(
        pack_kernel,
        [((16, 152, 128), BF)],
        core,
        kernel.reshape(16, 9, 256).transpose(1, 0, 2),
        channel_bias.reshape(1, 16),
        inputs,
        cotangent,
        hbm=(1, 2, 3, 4),
        copied=(0,),
        mib=56,
        scratch=[
            pltpu.VMEM((9, 16, 256), BF),
            pltpu.VMEM((1, 16), F32),
            pltpu.VMEM((16, 16, 384), BF),
            pltpu.VMEM((16, 16, 384), BF),
            pltpu.VMEM((16, 152, 128), BF),
            pltpu.SemaphoreType.DMA((4,)),
            pltpu.SemaphoreType.DMA((4,)),
        ],
    )
    got = lax.all_to_all(packed, SLOTS, 0, 0)
    xo, co, ha, w_part = call(
        unpack_kernel,
        [((768, 256), BF), ((512, 128), BF), ((96, 256), BF), ((16, 40, 128), BF)],
        core,
        got,
    )
    across = [(b, b + 1) for b in range(1, 15, 2)]
    across += [(b + 1, b) for b in range(1, 15, 2)]
    xr = lax.ppermute(xo, "core", [(0, 1), (1, 0)])
    ha = lax.ppermute(ha, BAND, across)
    hb = lax.ppermute(ha, "core", [(0, 1), (1, 0)])
    far = [(i, (i + 2) % 8) for i in range(8)] + [(8 + i, 8 + (i + 6) % 8) for i in range(8)]
    (w,) = call(
        weight_kernel,
        [((1152, 256), BF)],
        z,
        w_part,
        lax.ppermute(w_part, "z", [(i, (i + 1) % 8) for i in range(8)]),
        lax.ppermute(w_part, "z", [(i, (i + 7) % 8) for i in range(8)]),
        lax.ppermute(w_part, ("core", "z"), far),
        scratch=[pltpu.VMEM((4, 16, 40, 128), BF)],
    )
    scale = 1.0 / math.sqrt(256 * 384)

    def grads(*refs):
        grad_kernel(scale, *refs)

    kg, g = call(
        grads,
        [((16, 144, 128), BF), ((PX, 128), BF)],
        core,
        xo,
        xr,
        co,
        ha,
        hb,
        w,
        scratch=[
            pltpu.VMEM((1216, 256), BF),
            pltpu.VMEM((1088, 128), BF),
            pltpu.VMEM((PX, 384), F32),
            pltpu.VMEM((PX + 16, 128), F32),
            pltpu.VMEM((16, 144, 128), BF),
            pltpu.SemaphoreType.DMA((3,)),
        ],
        copied=(0,),
    )
    kg = lax.all_to_all(kg, SLOTS, 0, 0)
    own, send = call(
        input_kernel,
        [((512, 256), F32), ((512, 256), BF)],
        core,
        g,
        w,
        scratch=[pltpu.VMEM((3, 1056, 256), F32), pltpu.VMEM((1024, 256), F32)],
    )
    recv = lax.ppermute(send, "core", [(0, 1), (1, 0)])
    block = ((8, 48, 128), BF)
    keep, send = call(
        repack_kernel,
        [block, block],
        xh,
        own,
        recv,
        scratch=[pltpu.VMEM((8, 2, 48, 128), BF)],
    )
    recv = lax.ppermute(send, "xh", [(0, 1), (1, 0)])
    (joined,) = call(join_kernel, [((8, 96, 128), BF)], xh, keep, recv)
    back = lax.all_to_all(joined, "z", 0, 0)
    (input_grad,) = call(restore_kernel, [((16, 16, 384), BF)], back, smem=0)

    part = ((144, 128), BF)
    (sums,) = call(sum_kernel, [part], kg, joined, smem=0, hbm=(1,))
    ring = [lax.ppermute(sums, "y", [(i, (i + k) % 4) for i in range(4)]) for k in (3, 1, 2)]
    (sums,) = call(ring_kernel, [part], sums, *ring, smem=0)
    (ordered,) = call(
        order_kernel,
        [((9, 16, 256), F32)],
        core,
        sums,
        lax.ppermute(sums, "xl", [(0, 1), (1, 0)]),
        lax.ppermute(sums, "core", [(0, 1), (1, 0)]),
        lax.ppermute(sums, ("xl", "core"), [(i, i ^ 3) for i in range(4)]),
    )
    kernel_grad = ordered.transpose(1, 0, 2).reshape(16, 3, 3, 256)
    return (input_grad, kernel_grad)


def solution(mesh):
    fine = Mesh(mesh.devices.reshape(2, 4, 2, 8, 2), ("xl", "y", "core", "z", "xh"))
    return jax.shard_map(
        shards,
        mesh=fine,
        in_specs=(
            P(CHAN, BAND, None),
            P(CHAN, BAND, None),
            P(CHAN, None, None, None),
            P(CHAN),
        ),
        out_specs=(P(CHAN, BAND, None), P(CHAN, None, None, None)),
        check_vma=False,
    )
```

```python
import math

import jax
import jax.numpy as jnp
from jax import lax
from jax.experimental import pallas as pl
from jax.experimental.pallas import tpu as pltpu
from jax.sharding import Mesh
from jax.sharding import PartitionSpec as P

BF = jnp.bfloat16
F32 = jnp.float32
CHAN = ("z", "xh")
SLOTS = ("xh", "z")
BAND = ("xl", "y", "core")
PITCH = 32
NCOL = 24
PX = 1152
NT = (((1,), (1,)), ((), ()))
TN = (((0,), (0,)), ((), ()))


def dot(a, b, dims=(((1,), (0,)), ((), ()))):
    return lax.dot_general(a, b, dims, preferred_element_type=F32)


def iota(shape, dim):
    return lax.broadcasted_iota(jnp.int32, shape, dim)


def call(body, outs, *args, smem=1, scratch=(), hbm=(), copied=(), mib=48):
    specs = [
        pl.BlockSpec(
            memory_space=pltpu.SMEM if k < smem else pltpu.HBM if k in hbm else pltpu.VMEM
        )
        for k in range(len(args))
    ]
    return pl.pallas_call(
        body,
        out_shape=[jax.ShapeDtypeStruct(s, d) for s, d in outs],
        in_specs=specs,
        out_specs=[
            pl.BlockSpec(memory_space=pltpu.HBM if k in copied else pltpu.VMEM)
            for k in range(len(outs))
        ],
        scratch_shapes=list(scratch),
        compiler_params=pltpu.CompilerParams(vmem_limit_bytes=mib * 1024 * 1024),
    )(*args)


def swap_blocks(arrays, block):
    lanes = arrays[0].shape[1]
    place = iota(arrays[0].shape, 1) // block
    bit = 1
    while bit < len(arrays):
        upper = (place & bit) != 0
        out = list(arrays)
        for s in range(len(arrays)):
            if s & bit:
                continue
            a, b = arrays[s], arrays[s | bit]
            out[s] = jnp.where(upper, pltpu.roll(b, bit * block, 1), a)
            out[s | bit] = jnp.where(upper, b, pltpu.roll(a, lanes - bit * block, 1))
        arrays = out
        bit *= 2
    return arrays


def window(first, count):
    row = iota((512, 1), 0)
    c = row & 31
    column = jnp.where(c < count, (row >> 5) * NCOL + c + first, -1)
    return jnp.where(iota((512, 384), 1) == column, 1.0, 0.0).astype(BF)


def half_up(tile):
    return pltpu.roll(tile, 4, tile.ndim - 2)


def fold(field):
    low = iota((16, 8, 128), 1) < 4
    rest = jnp.where(low, field[:, 24:32, 0:128], half_up(field[:, 24:32, 128:256]))
    return [field[:, 0:24, 0:128], field[:, 0:24, 128:256], rest]


def unfold(chunk):
    rest = chunk[48:56]
    return [
        jnp.concatenate([chunk[0:24], rest], axis=0).astype(BF),
        jnp.concatenate([chunk[24:48], half_up(rest)], axis=0).astype(BF),
    ]


def copy_rows(buffer, out, first, last, sem):
    rows = pl.ds(first, last - first)
    copy = pltpu.make_async_copy(buffer.at[:, rows, :], out.at[:, rows, :], sem)
    copy.start()
    return copy


def pack_kernel(core_ref, *refs):
    out_hbm, buffer, sems, out_sems = refs[4], refs[9], refs[10], refs[11]
    copies = [pltpu.make_async_copy(refs[k], refs[5 + k], sems.at[k]) for k in range(4)]
    for copy in copies:
        copy.start()
    ker_ref, bias_ref, x_ref, cot_ref = refs[5:9]
    core = core_ref[0]
    dst = iota((256, 256), 0)
    src = iota((256, 256), 1)
    ch, h = src >> 4, src & 15
    to_h_ch = jnp.where(dst == h * 16 + ch, 1.0, 0.0).astype(BF)
    other = (ch >> 3) ^ core
    to_half = jnp.where(dst == other * 128 + h * 8 + (ch & 7), 1.0, 0.0).astype(BF)
    x_window = window(-2, 28)
    cot_window = window(-1, 26)

    copies[0].wait()
    upper = iota((8, 256), 0) < 4
    mine = []
    for t in range(9):
        both = ker_ref[t].astype(F32)
        mine.append(jnp.where(core == 0, both[0:8], both[8:16]))
    halves = []
    for r in range(2):
        taps = [mine[t] if (t % 2 == r) else half_up(mine[t]) for t in range(9)] + [mine[8]]
        pairs = [jnp.where(upper, taps[t], taps[t + 1]) for t in range(0, 10, 2)]
        halves.append(jnp.concatenate(pairs, axis=0))
    copies[1].wait()
    bias = jnp.broadcast_to(bias_ref[...], (8, 16))
    hi = bias.astype(BF).astype(F32)
    mid = (bias - hi).astype(BF).astype(F32)
    low = bias - hi - mid
    k = iota((8, 16), 0)
    pieces = jnp.where(k == 2, hi, jnp.where(k == 3, mid, jnp.where(k == 6, low, 0.0)))
    spread = iota((16, 128), 0) == (core * 8 + (iota((16, 128), 1) & 7))
    pieces = dot(pieces.astype(BF), jnp.where(spread, 1.0, 0.0).astype(BF))

    copies[2].wait()
    copies[3].wait()
    x = dot(to_h_ch, x_ref[...].reshape(256, 384)).astype(BF)
    x = fold(dot(x_window, x, NT).reshape(16, 32, 256))
    c = dot(to_half, cot_ref[...].reshape(256, 384)).astype(BF)
    c = fold(dot(cot_window, c, NT).reshape(16, 32, 256))
    c[2] = c[2] + pieces[None]
    field = jnp.concatenate(x + c, axis=1)
    sent = []
    for first in range(0, 16, 4):
        for k in range(first, first + 4):
            j = SOURCES[k]
            lane = (j // 2 % 2) * 128
            quarter = halves[j // 4 % 2][:, lane : lane + 128]
            buffer[k] = jnp.concatenate([field[j], quarter], axis=0).astype(BF)
        slabs = pl.ds(first, 4)
        copy = pltpu.make_async_copy(buffer.at[slabs], out_hbm.at[slabs], out_sems.at[first // 4])
        copy.start()
        sent.append(copy)
    for copy in sent:
        copy.wait()


SOURCES = [z * 2 + xh for xh in range(2) for z in range(8)]


def unpack_kernel(core_ref, r_ref, xo_ref, co_ref, ha_ref, w_ref):
    core = core_ref[0]
    edge = []
    chunks = [r_ref[s % 2 * 8 + s // 2].astype(F32) for s in range(16)]
    fields = [unfold(chunk[0:56]) for chunk in chunks]
    for hh in range(2):
        halves = []
        for sh in range(2):
            halves.append(swap_blocks([fields[sh * 8 + s][hh] for s in range(8)], 16))
        for hl in range(8):
            at = (hh * 8 + hl) * 32
            row = jnp.concatenate([halves[0][hl], halves[1][hl]], axis=1)
            xo_ref[at : at + 32, :] = row
            if (hh * 8 + hl) in (0, 1, 14, 15):
                edge.append(row)
    cots = [unfold(chunks[s][56:112]) for s in SOURCES]
    own = swap_blocks([cot[0] for cot in cots], 8)
    oth = swap_blocks([cot[1] for cot in cots], 8)
    for h in range(16):
        co_ref[h * 32 : h * 32 + 32, :] = own[h]
        at = 512 + (h % 8) * 32
        xo_ref[at : at + 32, (h // 8) * 128 : (h // 8) * 128 + 128] = oth[h]
    first = core == 0
    ha_ref[0:32, :] = jnp.where(first, edge[0], edge[2])
    ha_ref[32:64, :] = jnp.where(first, edge[1], edge[3])
    ha_ref[64:96, 0:128] = jnp.where(first, oth[0], oth[15])
    ha_ref[64:96, 128:256] = jnp.where(first, own[0], own[15])
    for k in range(16):
        w_ref[k] = chunks[SOURCES[k]][112:152].astype(BF)


def weight_kernel(z_ref, own_ref, below_ref, above_ref, far_ref, w_ref, quarters):
    for ref, offset in ((own_ref, 0), (below_ref, 3), (above_ref, 1), (far_ref, 2)):
        quarters[(z_ref[0] + offset) & 3] = ref[...]
    upper = iota((16, 8, 128), 1) < 4
    for ih in range(2):
        first, second = quarters[ih].astype(F32), quarters[2 + ih].astype(F32)
        for t in range(9):
            rows = slice((t // 2) * 8, (t // 2) * 8 + 8)
            if t % 2 == 0:
                tap = jnp.where(upper, first[:, rows], half_up(second[:, rows]))
            else:
                tap = jnp.where(upper, half_up(first[:, rows]), second[:, rows])
            w_ref[t * 128 : t * 128 + 128, ih * 128 : ih * 128 + 128] = tap.reshape(
                128, 128
            ).astype(BF)


def grad_kernel(scale, core_ref, xo_ref, xr_ref, co_ref, ha_ref, hb_ref, w_ref, *refs):
    kg_hbm, g_ref, x, cot, y, gs, buffer, sems = refs
    core = core_ref[0]
    first = core == 0
    mine = pl.multiple_of(core * 512, 512)
    theirs = pl.multiple_of((1 - core) * 512, 512)
    x[0:64, :] = jnp.where(first, ha_ref[0:64, :], hb_ref[0:64, :])
    x[pl.ds(64 + mine, 512), :] = xo_ref[0:512, :]
    x[pl.ds(64 + theirs, 512), :] = xr_ref[0:512, :]
    x[1088:1152, :] = jnp.where(first, hb_ref[0:64, :], ha_ref[0:64, :])
    x[1152:1216, :] = jnp.zeros((64, 256), BF)
    cot[0:32, :] = jnp.where(first, ha_ref[64:96, 0:128], hb_ref[64:96, 128:256])
    cot[pl.ds(32 + mine, 512), :] = co_ref[...]
    cot[pl.ds(32 + theirs, 256), :] = xr_ref[512:768, 0:128]
    cot[pl.ds(32 + theirs + 256, 256), :] = xr_ref[512:768, 128:256]
    cot[1056:1088, :] = jnp.where(first, hb_ref[64:96, 128:256], ha_ref[64:96, 0:128])

    bias = co_ref[16:32, :].astype(F32)
    bias = bias[10:11] + bias[11:12] + bias[14:15]

    for m in range(0, PX, 384):
        y[m : m + 384, :] = (
            dot(x[m : m + 384, :], w_ref[0:384, :], NT)
            + dot(x[m + 32 : m + 416, :], w_ref[384:768, :], NT)
            + dot(x[m + 64 : m + 448, :], w_ref[768:1152, :], NT)
        )

    gs[0:16, :] = jnp.zeros((16, 128), F32)
    for m in range(0, 1088, 64):
        pre = (
            y[m : m + 64, 0:128]
            + y[m + 1 : m + 65, 128:256]
            + y[m + 2 : m + 66, 256:384]
            + bias
        )
        s = 1.0 / (1.0 + jnp.exp(-pre))
        c = iota((64, 128), 0) & 31
        grad = cot[m : m + 64, :].astype(F32) * s * (1.0 + pre * (1.0 - s))
        grad = jnp.where(c < 26, grad, 0.0).astype(BF)
        g_ref[m : m + 64, :] = grad
        p = iota((64, 128), 0) + m
        inner = (c >= 1) & (c <= NCOL) & (p >= 32) & (p < 1056)
        gs[16 + m : 16 + m + 64, :] = jnp.where(inner, grad.astype(F32), 0.0)
    g_ref[1088:PX, :] = jnp.zeros((PX - 1088, 128), BF)
    gs[16 + 1088 : 16 + PX, :] = jnp.zeros((PX - 1088, 128), F32)

    shifted = jnp.concatenate(
        [gs[16 - b : 16 - b + PX, :].astype(BF) for b in range(3)], axis=1
    )
    sent = []
    for a in range(3):
        block = dot(shifted, x[32 * a : 32 * a + PX, :], TN) * scale
        for group in ((0, 1, 2),) if a < 2 else ((0,), (1,), (2,)):
            first, last = 48 * a + 16 * group[0], 48 * a + 16 * group[-1] + 16
            for k in range(16):
                rows = []
                for b in group:
                    tap = block[128 * b + 8 * k : 128 * b + 8 * k + 8]
                    rows += [tap[:, 0:128], tap[:, 128:256]]
                buffer[k, first:last, :] = jnp.concatenate(rows, axis=0).astype(BF)
            sent.append(copy_rows(buffer, kg_hbm, first, last, sems.at[len(sent)]))
    for copy in sent:
        copy.wait()


def input_kernel(core_ref, g_ref, w_ref, own_ref, send_ref, z, total):
    core = core_ref[0]
    for m in (0, 352, 704):
        for b in range(3):
            z[b, m : m + 352, :] = (
                dot(g_ref[m + 64 : m + 416, :], w_ref[b * 128 : b * 128 + 128, :])
                + dot(g_ref[m + 32 : m + 384, :], w_ref[384 + b * 128 : 512 + b * 128, :])
                + dot(g_ref[m : m + 352, :], w_ref[768 + b * 128 : 896 + b * 128, :])
            )
    for m in range(0, 1024, 64):
        total[m : m + 64, :] = (
            z[0, m + 2 : m + 66, :] + z[1, m + 1 : m + 65, :] + z[2, m : m + 64, :]
        )
    own_ref[...] = total[pl.ds(pl.multiple_of(core * 512, 512), 512), :]
    send_ref[...] = total[pl.ds(pl.multiple_of((1 - core) * 512, 512), 512), :].astype(BF)


def repack_kernel(xh_ref, own_ref, recv_ref, keep_ref, send_ref, chunks):
    parts = []
    for hh in range(2):
        rows = []
        for hl in range(8):
            at = (hh * 8 + hl) * 32
            row = own_ref[at : at + 32, :] + recv_ref[at : at + 32, :].astype(F32)
            rows.append(row[0:NCOL])
        parts.append([swap_blocks([r[:, q : q + 128] for r in rows], 16) for q in (0, 128)])
    for d in range(16):
        chunks[d // 2, d % 2] = jnp.concatenate(
            [parts[0][d // 8][d % 8], parts[1][d // 8][d % 8]], axis=0
        ).astype(BF)
    keep_ref[...] = chunks[:, pl.ds(xh_ref[0], 1)].reshape(8, 48, 128)
    send_ref[...] = chunks[:, pl.ds(1 - xh_ref[0], 1)].reshape(8, 48, 128)


def join_kernel(xh_ref, keep_ref, recv_ref, out_ref):
    first = xh_ref[0] == 0
    out_ref[:, 0:48, :] = jnp.where(first, keep_ref[...], recv_ref[...])
    out_ref[:, 48:96, :] = jnp.where(first, recv_ref[...], keep_ref[...])


def restore_kernel(r_ref, out_ref):
    halves = [[], []]
    for j in range(16):
        chunk = r_ref[j // 2, (j % 2) * 48 : (j % 2) * 48 + 48, :].astype(F32)
        halves[0].append(chunk[0:NCOL])
        halves[1].append(chunk[NCOL : 2 * NCOL])
    field = jnp.concatenate(
        [jnp.concatenate(half, axis=0) for half in halves], axis=1
    ).astype(BF)
    row = iota((256, 256), 0)
    pick = iota((256, 256), 1) == (row & 15) * 16 + (row >> 4)
    out = dot(jnp.where(pick, 1.0, 0.0).astype(BF), field, NT)
    out_ref[...] = out.astype(BF).reshape(16, 16, 384)


def sum_kernel(r_ref, after_ref, out_ref):
    total = r_ref[0].astype(F32)
    for s in range(1, 16):
        total = total + r_ref[s].astype(F32)
    out_ref[...] = total.astype(BF)


def ring_kernel(own_ref, next_ref, prev_ref, far_ref, out_ref):
    even = own_ref[...].astype(F32) + far_ref[...].astype(F32)
    odd = next_ref[...].astype(F32) + prev_ref[...].astype(F32)
    out_ref[...] = (even + odd).astype(BF)


def order_kernel(core_ref, own_ref, xl_ref, core_own_ref, core_xl_ref, out_ref):
    first = core_ref[0] == 0
    mine = own_ref[...].astype(F32) + xl_ref[...].astype(F32)
    other = core_own_ref[...].astype(F32) + core_xl_ref[...].astype(F32)
    low = jnp.where(first, mine, other)
    high = jnp.where(first, other, mine)
    for t in range(9):
        for ih in range(2):
            rows = slice((t * 2 + ih) * 8, (t * 2 + ih) * 8 + 8)
            out_ref[t, 0:8, ih * 128 : ih * 128 + 128] = low[rows]
            out_ref[t, 8:16, ih * 128 : ih * 128 + 128] = high[rows]


def shards(inputs, cotangent, kernel, channel_bias):
    core, z, xh = (
        lax.axis_index(n).astype(jnp.int32).reshape(1) for n in ("core", "z", "xh")
    )
    (packed,) = call(
        pack_kernel,
        [((16, 152, 128), BF)],
        core,
        kernel.reshape(16, 9, 256).transpose(1, 0, 2),
        channel_bias.reshape(1, 16),
        inputs,
        cotangent,
        hbm=(1, 2, 3, 4),
        copied=(0,),
        mib=56,
        scratch=[
            pltpu.VMEM((9, 16, 256), BF),
            pltpu.VMEM((1, 16), F32),
            pltpu.VMEM((16, 16, 384), BF),
            pltpu.VMEM((16, 16, 384), BF),
            pltpu.VMEM((16, 152, 128), BF),
            pltpu.SemaphoreType.DMA((4,)),
            pltpu.SemaphoreType.DMA((4,)),
        ],
    )
    got = lax.all_to_all(packed, SLOTS, 0, 0)
    xo, co, ha, w_part = call(
        unpack_kernel,
        [((768, 256), BF), ((512, 128), BF), ((96, 256), BF), ((16, 40, 128), BF)],
        core,
        got,
    )
    across = [(b, b + 1) for b in range(1, 15, 2)]
    across += [(b + 1, b) for b in range(1, 15, 2)]
    xr = lax.ppermute(xo, "core", [(0, 1), (1, 0)])
    ha = lax.ppermute(ha, BAND, across)
    hb = lax.ppermute(ha, "core", [(0, 1), (1, 0)])
    far = [(i, (i + 2) % 8) for i in range(8)] + [(8 + i, 8 + (i + 6) % 8) for i in range(8)]
    (w,) = call(
        weight_kernel,
        [((1152, 256), BF)],
        z,
        w_part,
        lax.ppermute(w_part, "z", [(i, (i + 1) % 8) for i in range(8)]),
        lax.ppermute(w_part, "z", [(i, (i + 7) % 8) for i in range(8)]),
        lax.ppermute(w_part, ("core", "z"), far),
        scratch=[pltpu.VMEM((4, 16, 40, 128), BF)],
    )
    scale = 1.0 / math.sqrt(256 * 384)

    def grads(*refs):
        grad_kernel(scale, *refs)

    kg, g = call(
        grads,
        [((16, 144, 128), BF), ((PX, 128), BF)],
        core,
        xo,
        xr,
        co,
        ha,
        hb,
        w,
        scratch=[
            pltpu.VMEM((1216, 256), BF),
            pltpu.VMEM((1088, 128), BF),
            pltpu.VMEM((PX, 384), F32),
            pltpu.VMEM((PX + 16, 128), F32),
            pltpu.VMEM((16, 144, 128), BF),
            pltpu.SemaphoreType.DMA((5,)),
        ],
        copied=(0,),
    )
    kg = lax.all_to_all(kg, SLOTS, 0, 0)
    own, send = call(
        input_kernel,
        [((512, 256), F32), ((512, 256), BF)],
        core,
        g,
        w,
        scratch=[pltpu.VMEM((3, 1056, 256), F32), pltpu.VMEM((1024, 256), F32)],
    )
    recv = lax.ppermute(send, "core", [(0, 1), (1, 0)])
    block = ((8, 48, 128), BF)
    keep, send = call(
        repack_kernel,
        [block, block],
        xh,
        own,
        recv,
        scratch=[pltpu.VMEM((8, 2, 48, 128), BF)],
    )
    recv = lax.ppermute(send, "xh", [(0, 1), (1, 0)])
    (joined,) = call(join_kernel, [((8, 96, 128), BF)], xh, keep, recv)
    back = lax.all_to_all(joined, "z", 0, 0)
    (input_grad,) = call(restore_kernel, [((16, 16, 384), BF)], back, smem=0)

    part = ((144, 128), BF)
    (sums,) = call(sum_kernel, [part], kg, joined, smem=0, hbm=(1,))
    ring = [lax.ppermute(sums, "y", [(i, (i + k) % 4) for i in range(4)]) for k in (3, 1, 2)]
    (sums,) = call(ring_kernel, [part], sums, *ring, smem=0)
    (ordered,) = call(
        order_kernel,
        [((9, 16, 256), F32)],
        core,
        sums,
        lax.ppermute(sums, "xl", [(0, 1), (1, 0)]),
        lax.ppermute(sums, "core", [(0, 1), (1, 0)]),
        lax.ppermute(sums, ("xl", "core"), [(i, i ^ 3) for i in range(4)]),
    )
    kernel_grad = ordered.transpose(1, 0, 2).reshape(16, 3, 3, 256)
    return (input_grad, kernel_grad)


def solution(mesh):
    fine = Mesh(mesh.devices.reshape(2, 4, 2, 8, 2), ("xl", "y", "core", "z", "xh"))
    return jax.shard_map(
        shards,
        mesh=fine,
        in_specs=(
            P(CHAN, BAND, None),
            P(CHAN, BAND, None),
            P(CHAN, None, None, None),
            P(CHAN),
        ),
        out_specs=(P(CHAN, BAND, None), P(CHAN, None, None, None)),
        check_vma=False,
    )
```

```python
import math

import jax
import jax.numpy as jnp
from jax import lax
from jax.experimental import pallas as pl
from jax.experimental.pallas import tpu as pltpu
from jax.sharding import Mesh
from jax.sharding import PartitionSpec as P

BF = jnp.bfloat16
F32 = jnp.float32
CHAN = ("z", "xh")
SLOTS = ("xh", "z")
BAND = ("xl", "y", "core")
PITCH = 32
NCOL = 24
PX = 1152
NT = (((1,), (1,)), ((), ()))
TN = (((0,), (0,)), ((), ()))


def dot(a, b, dims=(((1,), (0,)), ((), ()))):
    return lax.dot_general(a, b, dims, preferred_element_type=F32)


def iota(shape, dim):
    return lax.broadcasted_iota(jnp.int32, shape, dim)


def call(body, outs, *args, smem=1, scratch=(), hbm=(), copied=(), mib=48):
    specs = [
        pl.BlockSpec(
            memory_space=pltpu.SMEM if k < smem else pltpu.HBM if k in hbm else pltpu.VMEM
        )
        for k in range(len(args))
    ]
    return pl.pallas_call(
        body,
        out_shape=[jax.ShapeDtypeStruct(s, d) for s, d in outs],
        in_specs=specs,
        out_specs=[
            pl.BlockSpec(memory_space=pltpu.HBM if k in copied else pltpu.VMEM)
            for k in range(len(outs))
        ],
        scratch_shapes=list(scratch),
        compiler_params=pltpu.CompilerParams(vmem_limit_bytes=mib * 1024 * 1024),
    )(*args)


def swap_blocks(arrays, block):
    lanes = arrays[0].shape[1]
    place = iota(arrays[0].shape, 1) // block
    bit = 1
    while bit < len(arrays):
        upper = (place & bit) != 0
        out = list(arrays)
        for s in range(len(arrays)):
            if s & bit:
                continue
            a, b = arrays[s], arrays[s | bit]
            out[s] = jnp.where(upper, pltpu.roll(b, bit * block, 1), a)
            out[s | bit] = jnp.where(upper, b, pltpu.roll(a, lanes - bit * block, 1))
        arrays = out
        bit *= 2
    return arrays


def window(first, count):
    row = iota((512, 1), 0)
    c = row & 31
    column = jnp.where(c < count, (row >> 5) * NCOL + c + first, -1)
    return jnp.where(iota((512, 384), 1) == column, 1.0, 0.0).astype(BF)


def half_up(tile):
    return pltpu.roll(tile, 4, tile.ndim - 2)


def fold(field):
    low = iota((16, 8, 128), 1) < 4
    rest = jnp.where(low, field[:, 24:32, 0:128], half_up(field[:, 24:32, 128:256]))
    return [field[:, 0:24, 0:128], field[:, 0:24, 128:256], rest]


def unfold(chunk):
    rest = chunk[48:56]
    return [
        jnp.concatenate([chunk[0:24], rest], axis=0).astype(BF),
        jnp.concatenate([chunk[24:48], half_up(rest)], axis=0).astype(BF),
    ]


def copy_rows(buffer, out, first, last, sem):
    rows = pl.ds(first, last - first)
    copy = pltpu.make_async_copy(buffer.at[:, rows, :], out.at[:, rows, :], sem)
    copy.start()
    return copy


def pack_kernel(core_ref, *refs):
    out_hbm, buffer, sems, out_sems = refs[4], refs[9], refs[10], refs[11]
    copies = [pltpu.make_async_copy(refs[k], refs[5 + k], sems.at[k]) for k in range(4)]
    for copy in copies[2:] + copies[:2]:
        copy.start()
    ker_ref, bias_ref, x_ref, cot_ref = refs[5:9]
    core = core_ref[0]
    dst = iota((256, 256), 0)
    src = iota((256, 256), 1)
    ch, h = src >> 4, src & 15
    to_h_ch = jnp.where(dst == h * 16 + ch, 1.0, 0.0).astype(BF)
    other = (ch >> 3) ^ core
    to_half = jnp.where(dst == other * 128 + h * 8 + (ch & 7), 1.0, 0.0).astype(BF)
    x_window = window(-2, 28)
    cot_window = window(-1, 26)

    copies[0].wait()
    upper = iota((8, 256), 0) < 4
    mine = []
    for t in range(9):
        both = ker_ref[t].astype(F32)
        mine.append(jnp.where(core == 0, both[0:8], both[8:16]))
    halves = []
    for r in range(2):
        taps = [mine[t] if (t % 2 == r) else half_up(mine[t]) for t in range(9)] + [mine[8]]
        pairs = [jnp.where(upper, taps[t], taps[t + 1]) for t in range(0, 10, 2)]
        halves.append(jnp.concatenate(pairs, axis=0))
    copies[1].wait()
    bias = jnp.broadcast_to(bias_ref[...], (8, 16))
    hi = bias.astype(BF).astype(F32)
    mid = (bias - hi).astype(BF).astype(F32)
    low = bias - hi - mid
    k = iota((8, 16), 0)
    pieces = jnp.where(k == 2, hi, jnp.where(k == 3, mid, jnp.where(k == 6, low, 0.0)))
    spread = iota((16, 128), 0) == (core * 8 + (iota((16, 128), 1) & 7))
    pieces = dot(pieces.astype(BF), jnp.where(spread, 1.0, 0.0).astype(BF))

    copies[2].wait()
    copies[3].wait()
    x = dot(to_h_ch, x_ref[...].reshape(256, 384)).astype(BF)
    x = fold(dot(x_window, x, NT).reshape(16, 32, 256))
    c = dot(to_half, cot_ref[...].reshape(256, 384)).astype(BF)
    c = fold(dot(cot_window, c, NT).reshape(16, 32, 256))
    c[2] = c[2] + pieces[None]
    field = jnp.concatenate(x + c, axis=1)
    sent = []
    for first in range(0, 16, 4):
        for k in range(first, first + 4):
            j = SOURCES[k]
            lane = (j // 2 % 2) * 128
            quarter = halves[j // 4 % 2][:, lane : lane + 128]
            buffer[k] = jnp.concatenate([field[j], quarter], axis=0).astype(BF)
        slabs = pl.ds(first, 4)
        copy = pltpu.make_async_copy(buffer.at[slabs], out_hbm.at[slabs], out_sems.at[first // 4])
        copy.start()
        sent.append(copy)
    for copy in sent:
        copy.wait()


SOURCES = [z * 2 + xh for xh in range(2) for z in range(8)]


def unpack_kernel(core_ref, r_ref, xo_ref, co_ref, ha_ref, w_ref):
    core = core_ref[0]
    edge = []
    chunks = [r_ref[s % 2 * 8 + s // 2].astype(F32) for s in range(16)]
    fields = [unfold(chunk[0:56]) for chunk in chunks]
    for hh in range(2):
        halves = []
        for sh in range(2):
            halves.append(swap_blocks([fields[sh * 8 + s][hh] for s in range(8)], 16))
        for hl in range(8):
            at = (hh * 8 + hl) * 32
            row = jnp.concatenate([halves[0][hl], halves[1][hl]], axis=1)
            xo_ref[at : at + 32, :] = row
            if (hh * 8 + hl) in (0, 1, 14, 15):
                edge.append(row)
    cots = [unfold(chunks[s][56:112]) for s in SOURCES]
    own = swap_blocks([cot[0] for cot in cots], 8)
    oth = swap_blocks([cot[1] for cot in cots], 8)
    for h in range(16):
        co_ref[h * 32 : h * 32 + 32, :] = own[h]
        at = 512 + (h % 8) * 32
        xo_ref[at : at + 32, (h // 8) * 128 : (h // 8) * 128 + 128] = oth[h]
    first = core == 0
    ha_ref[0:32, :] = jnp.where(first, edge[0], edge[2])
    ha_ref[32:64, :] = jnp.where(first, edge[1], edge[3])
    ha_ref[64:96, 0:128] = jnp.where(first, oth[0], oth[15])
    ha_ref[64:96, 128:256] = jnp.where(first, own[0], own[15])
    for k in range(16):
        w_ref[k] = chunks[SOURCES[k]][112:152].astype(BF)


def weight_kernel(z_ref, own_ref, below_ref, above_ref, far_ref, w_ref, quarters):
    for ref, offset in ((own_ref, 0), (below_ref, 3), (above_ref, 1), (far_ref, 2)):
        quarters[(z_ref[0] + offset) & 3] = ref[...]
    upper = iota((16, 8, 128), 1) < 4
    for ih in range(2):
        first, second = quarters[ih].astype(F32), quarters[2 + ih].astype(F32)
        for t in range(9):
            rows = slice((t // 2) * 8, (t // 2) * 8 + 8)
            if t % 2 == 0:
                tap = jnp.where(upper, first[:, rows], half_up(second[:, rows]))
            else:
                tap = jnp.where(upper, half_up(first[:, rows]), second[:, rows])
            w_ref[t * 128 : t * 128 + 128, ih * 128 : ih * 128 + 128] = tap.reshape(
                128, 128
            ).astype(BF)


def grad_kernel(scale, core_ref, xo_ref, xr_ref, co_ref, ha_ref, hb_ref, w_ref, *refs):
    kg_hbm, g_ref, x, cot, y, gs, buffer, sems = refs
    core = core_ref[0]
    first = core == 0
    mine = pl.multiple_of(core * 512, 512)
    theirs = pl.multiple_of((1 - core) * 512, 512)
    x[0:64, :] = jnp.where(first, ha_ref[0:64, :], hb_ref[0:64, :])
    x[pl.ds(64 + mine, 512), :] = xo_ref[0:512, :]
    x[pl.ds(64 + theirs, 512), :] = xr_ref[0:512, :]
    x[1088:1152, :] = jnp.where(first, hb_ref[0:64, :], ha_ref[0:64, :])
    x[1152:1216, :] = jnp.zeros((64, 256), BF)
    cot[0:32, :] = jnp.where(first, ha_ref[64:96, 0:128], hb_ref[64:96, 128:256])
    cot[pl.ds(32 + mine, 512), :] = co_ref[...]
    cot[pl.ds(32 + theirs, 256), :] = xr_ref[512:768, 0:128]
    cot[pl.ds(32 + theirs + 256, 256), :] = xr_ref[512:768, 128:256]
    cot[1056:1088, :] = jnp.where(first, hb_ref[64:96, 128:256], ha_ref[64:96, 0:128])

    bias = co_ref[16:32, :].astype(F32)
    bias = bias[10:11] + bias[11:12] + bias[14:15]

    for m in range(0, PX, 384):
        y[m : m + 384, :] = (
            dot(x[m : m + 384, :], w_ref[0:384, :], NT)
            + dot(x[m + 32 : m + 416, :], w_ref[384:768, :], NT)
            + dot(x[m + 64 : m + 448, :], w_ref[768:1152, :], NT)
        )

    gs[0:16, :] = jnp.zeros((16, 128), F32)
    for m in range(0, 1088, 64):
        pre = (
            y[m : m + 64, 0:128]
            + y[m + 1 : m + 65, 128:256]
            + y[m + 2 : m + 66, 256:384]
            + bias
        )
        s = 1.0 / (1.0 + jnp.exp(-pre))
        c = iota((64, 128), 0) & 31
        grad = cot[m : m + 64, :].astype(F32) * s * (1.0 + pre * (1.0 - s))
        grad = jnp.where(c < 26, grad, 0.0).astype(BF)
        g_ref[m : m + 64, :] = grad
        p = iota((64, 128), 0) + m
        inner = (c >= 1) & (c <= NCOL) & (p >= 32) & (p < 1056)
        gs[16 + m : 16 + m + 64, :] = jnp.where(inner, grad.astype(F32), 0.0)
    g_ref[1088:PX, :] = jnp.zeros((PX - 1088, 128), BF)
    gs[16 + 1088 : 16 + PX, :] = jnp.zeros((PX - 1088, 128), F32)

    shifted = jnp.concatenate(
        [gs[16 - b : 16 - b + PX, :].astype(BF) for b in range(3)], axis=1
    )
    sent = []
    for a in range(3):
        block = dot(shifted, x[32 * a : 32 * a + PX, :], TN) * scale
        for group in ((0, 1, 2),) if a < 2 else ((0,), (1,), (2,)):
            first, last = 48 * a + 16 * group[0], 48 * a + 16 * group[-1] + 16
            for k in range(16):
                rows = []
                for b in group:
                    tap = block[128 * b + 8 * k : 128 * b + 8 * k + 8]
                    rows += [tap[:, 0:128], tap[:, 128:256]]
                buffer[k, first:last, :] = jnp.concatenate(rows, axis=0).astype(BF)
            sent.append(copy_rows(buffer, kg_hbm, first, last, sems.at[len(sent)]))
    for copy in sent:
        copy.wait()


def input_kernel(core_ref, g_ref, w_ref, own_ref, send_ref, z, total):
    core = core_ref[0]
    for m in (0, 352, 704):
        for b in range(3):
            z[b, m : m + 352, :] = (
                dot(g_ref[m + 64 : m + 416, :], w_ref[b * 128 : b * 128 + 128, :])
                + dot(g_ref[m + 32 : m + 384, :], w_ref[384 + b * 128 : 512 + b * 128, :])
                + dot(g_ref[m : m + 352, :], w_ref[768 + b * 128 : 896 + b * 128, :])
            )
    for m in range(0, 1024, 64):
        total[m : m + 64, :] = (
            z[0, m + 2 : m + 66, :] + z[1, m + 1 : m + 65, :] + z[2, m : m + 64, :]
        )
    own_ref[...] = total[pl.ds(pl.multiple_of(core * 512, 512), 512), :]
    send_ref[...] = total[pl.ds(pl.multiple_of((1 - core) * 512, 512), 512), :].astype(BF)


def repack_kernel(xh_ref, own_ref, recv_ref, keep_ref, send_ref, chunks):
    parts = []
    for hh in range(2):
        rows = []
        for hl in range(8):
            at = (hh * 8 + hl) * 32
            row = own_ref[at : at + 32, :] + recv_ref[at : at + 32, :].astype(F32)
            rows.append(row[0:NCOL])
        parts.append([swap_blocks([r[:, q : q + 128] for r in rows], 16) for q in (0, 128)])
    for d in range(16):
        chunks[d // 2, d % 2] = jnp.concatenate(
            [parts[0][d // 8][d % 8], parts[1][d // 8][d % 8]], axis=0
        ).astype(BF)
    keep_ref[...] = chunks[:, pl.ds(xh_ref[0], 1)].reshape(8, 48, 128)
    send_ref[...] = chunks[:, pl.ds(1 - xh_ref[0], 1)].reshape(8, 48, 128)


def join_kernel(xh_ref, keep_ref, recv_ref, out_ref):
    first = xh_ref[0] == 0
    out_ref[:, 0:48, :] = jnp.where(first, keep_ref[...], recv_ref[...])
    out_ref[:, 48:96, :] = jnp.where(first, recv_ref[...], keep_ref[...])


def restore_kernel(r_ref, out_ref):
    halves = [[], []]
    for j in range(16):
        chunk = r_ref[j // 2, (j % 2) * 48 : (j % 2) * 48 + 48, :].astype(F32)
        halves[0].append(chunk[0:NCOL])
        halves[1].append(chunk[NCOL : 2 * NCOL])
    field = jnp.concatenate(
        [jnp.concatenate(half, axis=0) for half in halves], axis=1
    ).astype(BF)
    row = iota((256, 256), 0)
    pick = iota((256, 256), 1) == (row & 15) * 16 + (row >> 4)
    out = dot(jnp.where(pick, 1.0, 0.0).astype(BF), field, NT)
    out_ref[...] = out.astype(BF).reshape(16, 16, 384)


def sum_kernel(r_ref, after_ref, out_ref):
    total = r_ref[0].astype(F32)
    for s in range(1, 16):
        total = total + r_ref[s].astype(F32)
    out_ref[...] = total.astype(BF)


def ring_kernel(own_ref, next_ref, prev_ref, far_ref, out_ref):
    even = own_ref[...].astype(F32) + far_ref[...].astype(F32)
    odd = next_ref[...].astype(F32) + prev_ref[...].astype(F32)
    out_ref[...] = (even + odd).astype(BF)


def order_kernel(core_ref, own_ref, xl_ref, core_own_ref, core_xl_ref, out_ref):
    first = core_ref[0] == 0
    mine = own_ref[...].astype(F32) + xl_ref[...].astype(F32)
    other = core_own_ref[...].astype(F32) + core_xl_ref[...].astype(F32)
    low = jnp.where(first, mine, other)
    high = jnp.where(first, other, mine)
    for t in range(9):
        for ih in range(2):
            rows = slice((t * 2 + ih) * 8, (t * 2 + ih) * 8 + 8)
            out_ref[t, 0:8, ih * 128 : ih * 128 + 128] = low[rows]
            out_ref[t, 8:16, ih * 128 : ih * 128 + 128] = high[rows]


def shards(inputs, cotangent, kernel, channel_bias):
    core, z, xh = (
        lax.axis_index(n).astype(jnp.int32).reshape(1) for n in ("core", "z", "xh")
    )
    (packed,) = call(
        pack_kernel,
        [((16, 152, 128), BF)],
        core,
        kernel.reshape(16, 9, 256).transpose(1, 0, 2),
        channel_bias.reshape(1, 16),
        inputs,
        cotangent,
        hbm=(1, 2, 3, 4),
        copied=(0,),
        mib=56,
        scratch=[
            pltpu.VMEM((9, 16, 256), BF),
            pltpu.VMEM((1, 16), F32),
            pltpu.VMEM((16, 16, 384), BF),
            pltpu.VMEM((16, 16, 384), BF),
            pltpu.VMEM((16, 152, 128), BF),
            pltpu.SemaphoreType.DMA((4,)),
            pltpu.SemaphoreType.DMA((4,)),
        ],
    )
    got = lax.all_to_all(packed, SLOTS, 0, 0)
    xo, co, ha, w_part = call(
        unpack_kernel,
        [((768, 256), BF), ((512, 128), BF), ((96, 256), BF), ((16, 40, 128), BF)],
        core,
        got,
    )
    across = [(b, b + 1) for b in range(1, 15, 2)]
    across += [(b + 1, b) for b in range(1, 15, 2)]
    xr = lax.ppermute(xo, "core", [(0, 1), (1, 0)])
    ha = lax.ppermute(ha, BAND, across)
    hb = lax.ppermute(ha, "core", [(0, 1), (1, 0)])
    far = [(i, (i + 2) % 8) for i in range(8)] + [(8 + i, 8 + (i + 6) % 8) for i in range(8)]
    (w,) = call(
        weight_kernel,
        [((1152, 256), BF)],
        z,
        w_part,
        lax.ppermute(w_part, "z", [(i, (i + 1) % 8) for i in range(8)]),
        lax.ppermute(w_part, "z", [(i, (i + 7) % 8) for i in range(8)]),
        lax.ppermute(w_part, ("core", "z"), far),
        scratch=[pltpu.VMEM((4, 16, 40, 128), BF)],
    )
    scale = 1.0 / math.sqrt(256 * 384)

    def grads(*refs):
        grad_kernel(scale, *refs)

    kg, g = call(
        grads,
        [((16, 144, 128), BF), ((PX, 128), BF)],
        core,
        xo,
        xr,
        co,
        ha,
        hb,
        w,
        scratch=[
            pltpu.VMEM((1216, 256), BF),
            pltpu.VMEM((1088, 128), BF),
            pltpu.VMEM((PX, 384), F32),
            pltpu.VMEM((PX + 16, 128), F32),
            pltpu.VMEM((16, 144, 128), BF),
            pltpu.SemaphoreType.DMA((5,)),
        ],
        copied=(0,),
    )
    kg = lax.all_to_all(kg, SLOTS, 0, 0)
    own, send = call(
        input_kernel,
        [((512, 256), F32), ((512, 256), BF)],
        core,
        g,
        w,
        scratch=[pltpu.VMEM((3, 1056, 256), F32), pltpu.VMEM((1024, 256), F32)],
    )
    recv = lax.ppermute(send, "core", [(0, 1), (1, 0)])
    block = ((8, 48, 128), BF)
    keep, send = call(
        repack_kernel,
        [block, block],
        xh,
        own,
        recv,
        scratch=[pltpu.VMEM((8, 2, 48, 128), BF)],
    )
    recv = lax.ppermute(send, "xh", [(0, 1), (1, 0)])
    (joined,) = call(join_kernel, [((8, 96, 128), BF)], xh, keep, recv)
    back = lax.all_to_all(joined, "z", 0, 0)
    (input_grad,) = call(restore_kernel, [((16, 16, 384), BF)], back, smem=0)

    part = ((144, 128), BF)
    (sums,) = call(sum_kernel, [part], kg, joined, smem=0, hbm=(1,))
    ring = [lax.ppermute(sums, "y", [(i, (i + k) % 4) for i in range(4)]) for k in (3, 1, 2)]
    (sums,) = call(ring_kernel, [part], sums, *ring, smem=0)
    (ordered,) = call(
        order_kernel,
        [((9, 16, 256), F32)],
        core,
        sums,
        lax.ppermute(sums, "xl", [(0, 1), (1, 0)]),
        lax.ppermute(sums, "core", [(0, 1), (1, 0)]),
        lax.ppermute(sums, ("xl", "core"), [(i, i ^ 3) for i in range(4)]),
    )
    kernel_grad = ordered.transpose(1, 0, 2).reshape(16, 3, 3, 256)
    return (input_grad, kernel_grad)


def solution(mesh):
    fine = Mesh(mesh.devices.reshape(2, 4, 2, 8, 2), ("xl", "y", "core", "z", "xh"))
    return jax.shard_map(
        shards,
        mesh=fine,
        in_specs=(
            P(CHAN, BAND, None),
            P(CHAN, BAND, None),
            P(CHAN, None, None, None),
            P(CHAN),
        ),
        out_specs=(P(CHAN, BAND, None), P(CHAN, None, None, None)),
        check_vma=False,
    )
```
